32 devices in a mesh: cell: 8 (over z, x), spec: 4 (over y, core).
Axes of the slice: x: 2, y: 2, z: 4, core: 2. Of those that a mesh axis runs over, the one named last changes fastest.
Arguments:
- fields: bfloat16 [4, 256, 384], P('spec', 'cell'), may hold values from -6 to 6
- tensors: bfloat16 [16, 384, 384, 384], P('spec', 'cell'), may hold values from -0.0078125 to 0.0078125
- pair_table: int32 [4, 4], replicated, may hold values from 0 to 15, as said below
- plus_flux: float32 [4, 384, 384], P('spec'), may hold values from -0.3125 to 0.3125
- minus_flux: float32 [4, 384, 384], P('spec'), may hold values from -0.3125 to 0.3125
- face_limiter: int32 [4, 256], P('spec', 'cell'), may hold values from 0 to 2
Outputs:
- new_field: float32 [4, 256, 384], P('spec', 'cell')
- collision: float32 [4, 256, 384], P('spec', 'cell')
The draws below stay inside these ranges and needn't reach their ends.
Inputs may be any that keep to these rules, and one draw needn't show every extreme that they name: Row s of pair_table names each of the tensors s * 4 to s * 4 + 3 exactly once. `face_limiter`: 0 first order, 1 minmod slope, 2 monotonized central slope.
All inputs are finite; a program needn't handle non-finite values.
Results may differ from the reference program's by a relative error of at most 0.0004.
Values may be sent and summed in bfloat16 or wider, within the bound.
No kernel may reach another device: no remote copies, remote signals or barrier semaphores. Data moves between devices by JAX's collectives and lax.ppermute only.
A program may use at most 128 MiB of HBM per device.

```python
import math
import jax
import jax.numpy as jnp
from jax import lax

M = 384
SPEC = 4
NPAIR = 16
NCELL = 256


def draw_pair_table(key, part):
    keys = jax.random.split(jax.random.fold_in(key, 17), SPEC)
    orders = jax.vmap(lambda single: jax.random.permutation(single, SPEC))(keys)
    base = jnp.arange(SPEC, dtype=jnp.int32)[:, None] * SPEC
    return (base + orders.astype(jnp.int32)).astype(jnp.int32)


def touch_ends(entries, rng, low, high):
    longest = entries.shape.index(max(entries.shape))
    spots = []
    for shift in (0, 1):
        where = [jax.random.randint(jax.random.fold_in(rng, axis), (), 0, length) for axis, length in enumerate(entries.shape)]
        where[longest] = (where[longest] + shift) % entries.shape[longest]
        spots.append(tuple(where))
    return entries.at[spots[0]].set(low).at[spots[1]].set(high)


def block_scale(own_key, dims, shards, low, high):
    def one(position, parts):
        steps = jax.random.uniform(jax.random.fold_in(jax.random.fold_in(own_key, 6), position), (parts,), jnp.float32, low / len(shards), high / len(shards))
        return jnp.repeat(jnp.exp(steps), dims[position] // parts).reshape((-1,) + (1,) * (len(dims) - position - 1))

    gain = one(*shards[0])
    for cut in shards[1:]:
        gain = gain * one(*cut)
    return gain


def gaussian(own_key, shape, scale, reach, shards=(), held_as=jnp.bfloat16):
    entries = jax.random.normal(own_key, shape, jnp.float32) * scale
    if len(shards) > 0:
        entries = block_scale(own_key, shape, shards, -0.22, 0.18) * entries
    return jnp.clip(entries, min=-reach, max=reach).astype(held_as)


def setup_inputs(seed: int = 0) -> dict:
    streams_of = jax.random.split(jax.random.key(seed), 7)
    fields = gaussian(streams_of[0], (SPEC, NCELL, M), 1.0, 6.0, ((0, 4), (1, 8)))
    tensors = gaussian(streams_of[1], (NPAIR, M, M, M), (SPEC * M * M) ** -0.5, 0.0078125, ((0, 4), (1, 8)))
    pair_table = draw_pair_table(jax.random.fold_in(streams_of[6], 71), 0)
    plus_flux = gaussian(streams_of[3], (SPEC, M, M), M ** -0.5, 0.3125, ((0, 4),), jnp.float32)
    minus_flux = gaussian(streams_of[4], (SPEC, M, M), M ** -0.5, 0.3125, ((0, 4),), jnp.float32)
    face_limiter = touch_ends(jax.random.randint(streams_of[5], (SPEC, NCELL), 0, 3), jax.random.fold_in(streams_of[5], 1), 0, 2).astype(jnp.int32)
    return dict(fields=fields, tensors=tensors, pair_table=pair_table, plus_flux=plus_flux, minus_flux=minus_flux, face_limiter=face_limiter)


def minmod_two(first, second):
    return jnp.where(first * second > 0, jnp.sign(first) * jnp.minimum(jnp.abs(first), jnp.abs(second)), 0.0)


def minmod_three(first, second, third):
    same = (first * second > 0) & (second * third > 0)
    least = jnp.minimum(jnp.minimum(jnp.abs(first), jnp.abs(second)), jnp.abs(third))
    return jnp.where(same, jnp.sign(first) * least, 0.0)


def collide(fields, tensors, pair_table):
    block = math.gcd(NCELL, 32)
    field32 = fields.astype(jnp.float32)
    blocked = field32.reshape(SPEC, NCELL // block, block, M)
    results = []
    for owner in range(SPEC):
        total = jnp.zeros((NCELL // block, block, M), jnp.float32)
        for partner in range(SPEC):
            tensor = lax.dynamic_index_in_dim(tensors, pair_table[owner, partner], 0, keepdims=False).astype(jnp.float32)

            def one_block(pieces):
                own_piece, partner_piece = pieces
                inner = jnp.einsum("cj,kij->cki", partner_piece, tensor)
                return jnp.einsum("cki,ci->ck", inner, own_piece)

            total = total + lax.map(one_block, (blocked[owner], blocked[partner]))
        results.append(total.reshape(NCELL, M))
    return jnp.stack(results)


def reference(fields, tensors, pair_table, plus_flux, minus_flux, face_limiter):
    collision = collide(fields, tensors, pair_table)
    field32 = fields.astype(jnp.float32)
    before = jnp.roll(field32, 1, axis=1)
    after = jnp.roll(field32, -1, axis=1)
    lower = field32 - before
    upper = after - field32
    slope_one = minmod_two(lower, upper)
    slope_two = minmod_three(2.0 * lower, 0.5 * (lower + upper), 2.0 * upper)
    flags = face_limiter[:, :, None]
    zero = jnp.zeros_like(slope_one)
    here = jnp.where(flags == 1, slope_one, jnp.where(flags == 2, slope_two, zero))
    slope_one_next = jnp.roll(slope_one, -1, axis=1)
    slope_two_next = jnp.roll(slope_two, -1, axis=1)
    there = jnp.where(flags == 1, slope_one_next, jnp.where(flags == 2, slope_two_next, zero))
    left_state = field32 + 0.5 * here
    right_state = after - 0.5 * there
    flux = jnp.einsum("scm,smn->scn", left_state, plus_flux, precision=lax.Precision.HIGHEST)
    flux = flux + jnp.einsum("scm,smn->scn", right_state, minus_flux, precision=lax.Precision.HIGHEST)
    new_field = field32 + 0.4 * (jnp.roll(flux, 1, axis=1) - flux) + 0.5 * collision
    return new_field, collision
```

```python
import functools

import jax
import jax.numpy as jnp
from jax import lax
from jax.experimental import pallas as pl
from jax.experimental.pallas import tpu as pltpu
from jax.sharding import PartitionSpec as P

LANES = 128
MIB = 1 << 20


def minmod_two(first, second):
    least = jnp.minimum(jnp.abs(first), jnp.abs(second))
    return jnp.where(first * second > 0, jnp.where(first > 0, least, -least), 0.0)


def minmod_three(first, second, third):
    same = (first * second > 0) & (second * third > 0)
    least = jnp.minimum(jnp.minimum(jnp.abs(first), jnp.abs(second)), jnp.abs(third))
    return jnp.where(same, jnp.where(first > 0, least, -least), 0.0)


def column(row):
    n = row.shape[1]
    down = lax.broadcasted_iota(jnp.int32, (n, n), 0)
    across = lax.broadcasted_iota(jnp.int32, (n, n), 1)
    return jnp.sum(jnp.where(down == across, row, 0), axis=1, keepdims=True)


def fold_of(cells, out_modes):
    fold = 1
    while cells % (2 * fold) == 0 and 2 * fold * out_modes < LANES:
        fold *= 2
    return fold


def collide_kernel(place, order, gathered, tensors, limiter, out, other, own, total):
    step = pl.program_id(0)
    groups, species, cells, modes = gathered.shape
    block = tensors.shape[1]

    @pl.when(step == 0)
    def _():
        for p in range(species):
            rows = gathered[:, pl.ds(order[p], 1)].reshape(groups * cells, modes)
            other[p * modes : (p + 1) * modes, :] = rows.astype(jnp.float32).T.astype(other.dtype)
        rows = gathered[:, pl.ds(place[1], 1)].reshape(groups * cells, modes)
        own[...] = rows.astype(jnp.float32).T

    for k in range(block):
        left = jnp.concatenate([tensors[p, k] for p in range(species)], axis=1)
        inner = jnp.dot(left, other[...], preferred_element_type=jnp.float32)
        total[pl.ds(step * block + k, 1), :] = jnp.sum(inner * own[...], axis=0, keepdims=True)

    @pl.when(step == pl.num_programs(0) - 1)
    def _():
        whole = total[...].T
        out_modes = whole.shape[1]
        fold = fold_of(cells, out_modes)
        rows = cells // fold
        flag = limiter[:, cells - 1 :].astype(jnp.float32)
        spare = jnp.broadcast_to(flag, (rows, LANES - fold * out_modes))
        for d in range(groups):
            first = d * cells
            parts = [whole[first + f * rows : first + (f + 1) * rows] for f in range(fold)]
            out[d] = jnp.concatenate(parts + [spare], axis=1)


def collide(place, order, gathered, tensors, limiter):
    groups, species, cells, modes = gathered.shape
    out_modes = tensors.shape[1]
    rows = cells // fold_of(cells, out_modes)
    block = 2 if out_modes % 2 == 0 else 1
    return pl.pallas_call(
        collide_kernel,
        grid_spec=pltpu.PrefetchScalarGridSpec(
            num_scalar_prefetch=2,
            grid=(out_modes // block,),
            in_specs=[
                pl.BlockSpec(memory_space=pltpu.VMEM),
                pl.BlockSpec((species, block, modes, modes), lambda step, *_: (0, step, 0, 0)),
                pl.BlockSpec(memory_space=pltpu.VMEM),
            ],
            out_specs=pl.BlockSpec(memory_space=pltpu.VMEM),
            scratch_shapes=[
                pltpu.VMEM((species * modes, groups * cells), jnp.bfloat16),
                pltpu.VMEM((modes, groups * cells), jnp.float32),
                pltpu.VMEM((out_modes, groups * cells), jnp.float32),
            ],
        ),
        out_shape=jax.ShapeDtypeStruct((groups, rows, LANES), jnp.float32),
        compiler_params=pltpu.CompilerParams(vmem_limit_bytes=32 * MIB),
        name="collide",
    )(place, order, gathered, tensors, limiter)


def flux_kernel(place, gathered, limiter, plus, minus, flux):
    groups, species, cells, modes = gathered.shape
    here, owner = place[0], place[1]
    before = lax.rem(here + groups - 1, groups)
    after = lax.rem(here + 1, groups)
    wide = jnp.concatenate(
        [gathered[g, owner].astype(jnp.float32) for g in (before, here, after)], axis=0
    )
    wide = wide[cells - 2 : 2 * cells + 2]
    lower = wide[1:-1] - wide[:-2]
    upper = wide[2:] - wide[1:-1]
    one = minmod_two(lower, upper)
    two = minmod_three(2.0 * lower, 0.5 * (lower + upper), 2.0 * upper)
    flags = column(limiter[...])
    ahead = lax.broadcasted_iota(jnp.int32, (3, 1), 0)

    def chosen(first, second, flag):
        return jnp.where(flag == 1, first, jnp.where(flag == 2, second, 0.0))

    def stack(shift):
        base = wide[1 + shift :]
        faces = base[1 : cells + 1]
        faces = faces + (0.5 - shift) * chosen(
            one[1 + shift : 1 + shift + cells], two[1 + shift : 1 + shift + cells], flags
        )
        edge = base[:1] + (0.5 - shift) * chosen(
            one[shift : shift + 1], two[shift : shift + 1], ahead
        )
        pad = jnp.zeros((flux.shape[0] - cells - 3, modes), jnp.float32)
        return jnp.concatenate([faces, edge, pad], axis=0)

    total = jnp.dot(
        stack(0), plus[0], precision=lax.Precision.HIGHEST, preferred_element_type=jnp.float32
    )
    total = total + jnp.dot(
        stack(1), minus[0], precision=lax.Precision.HIGHEST, preferred_element_type=jnp.float32
    )
    flux[...] = total


def transport(place, gathered, limiter, plus, minus):
    groups, species, cells, modes = gathered.shape
    vmem = pl.BlockSpec(memory_space=pltpu.VMEM)
    return pl.pallas_call(
        flux_kernel,
        in_specs=[pl.BlockSpec(memory_space=pltpu.SMEM), vmem, vmem, vmem, vmem],
        out_specs=vmem,
        out_shape=jax.ShapeDtypeStruct((cells + 8, modes), jnp.float32),
        compiler_params=pltpu.CompilerParams(vmem_limit_bytes=16 * MIB),
        name="transport",
    )(place, gathered, limiter, plus, minus)


def finish_kernel(out_modes, place, received, flux, fields, new_field, collision):
    groups, rows, _ = received.shape
    cells = fields.shape[1]
    fold = cells // rows
    parts = []
    for f in range(fold):
        pieces = [received[g][:, f * out_modes : (f + 1) * out_modes] for g in range(groups)]
        parts.append(jnp.concatenate(pieces, axis=1))
    term = jnp.concatenate(parts, axis=0)
    collision[0] = term
    before = lax.rem(place[0] + groups - 1, groups)
    flag = received[before][:1, fold * out_modes : fold * out_modes + 1]
    behind = flux[cells : cells + 3]
    edge = jnp.where(flag == 1.0, behind[1:2], jnp.where(flag == 2.0, behind[2:3], behind[:1]))
    faces = flux[:cells]
    ahead = jnp.concatenate([edge, faces[:-1]], axis=0)
    new_field[0] = fields[0].astype(jnp.float32) + 0.4 * (ahead - faces) + 0.5 * term


def finish(place, received, flux, fields, out_modes):
    vmem = pl.BlockSpec(memory_space=pltpu.VMEM)
    shape = jax.ShapeDtypeStruct(fields.shape, jnp.float32)
    return pl.pallas_call(
        functools.partial(finish_kernel, out_modes),
        in_specs=[pl.BlockSpec(memory_space=pltpu.SMEM), vmem, vmem, vmem],
        out_specs=(vmem, vmem),
        out_shape=(shape, shape),
        compiler_params=pltpu.CompilerParams(vmem_limit_bytes=16 * MIB),
        name="finish",
    )(place, received, flux, fields)


def local(fields, tensors, pair_table, plus_flux, minus_flux, face_limiter):
    species = lax.axis_size("spec")
    owner = lax.axis_index("spec")
    position = lax.axis_index("cell")
    place = jnp.stack([position, owner]).astype(jnp.int32)
    row = lax.dynamic_index_in_dim(pair_table, owner, 0, keepdims=False) - owner * species
    order = jnp.sum(
        jnp.where(row[None, :] == jnp.arange(species)[:, None], jnp.arange(species)[None, :], 0),
        axis=1,
        dtype=jnp.int32,
    )
    everyone = lax.all_gather(fields[0], ("cell", "spec"), axis=0, tiled=False)
    gathered = everyone.reshape((lax.axis_size("cell"), species) + fields.shape[1:])
    block = collide(place, order, gathered, tensors, face_limiter)
    received = lax.all_to_all(block, "cell", split_axis=0, concat_axis=0, tiled=False)
    flux = transport(place, gathered, face_limiter, plus_flux, minus_flux)
    return finish(place, received, flux, fields, tensors.shape[1])


def solution(mesh):
    placed = (
        P("spec", "cell", None),
        P("spec", "cell", None, None),
        P(),
        P("spec", None, None),
        P("spec", None, None),
        P("spec", "cell"),
    )
    return jax.shard_map(
        local,
        mesh=mesh,
        in_specs=placed,
        out_specs=(P("spec", "cell", None), P("spec", "cell", None)),
        check_vma=False,
    )
```

```python
import functools

import jax
import jax.numpy as jnp
from jax import lax
from jax.experimental import pallas as pl
from jax.experimental.pallas import tpu as pltpu
from jax.sharding import PartitionSpec as P

LANES = 128
MIB = 1 << 20


def minmod_two(first, second):
    least = jnp.minimum(jnp.abs(first), jnp.abs(second))
    return jnp.where(first * second > 0, jnp.where(first > 0, least, -least), 0.0)


def minmod_three(first, second, third):
    same = (first * second > 0) & (second * third > 0)
    least = jnp.minimum(jnp.minimum(jnp.abs(first), jnp.abs(second)), jnp.abs(third))
    return jnp.where(same, jnp.where(first > 0, least, -least), 0.0)


def column(row):
    n = row.shape[1]
    down = lax.broadcasted_iota(jnp.int32, (n, n), 0)
    across = lax.broadcasted_iota(jnp.int32, (n, n), 1)
    return jnp.sum(jnp.where(down == across, row, 0), axis=1, keepdims=True)


def fold_of(cells, out_modes):
    fold = 1
    while cells % (2 * fold) == 0 and 2 * fold * out_modes < LANES:
        fold *= 2
    return fold


def collide_kernel(
    table, *refs, species
):
    spread = refs[:species]
    tensors, limiter, out, other, own, total = refs[species:]
    step = pl.program_id(0)
    groups, cells, modes = spread[0].shape
    block = tensors.shape[1]
    everyone = groups * cells
    width = 2 * LANES
    owner = lax.axis_index("spec")

    @pl.when(step == 0)
    def _():
        for q in range(species):
            p = table[owner, owner ^ q] - owner * species
            other[p] = spread[q][...].reshape(everyone, modes)
        own[...] = spread[0][...].reshape(everyone, modes).astype(jnp.float32).T

    def strip(ref, lead, rows, tile):
        parts = []
        for piece in range(2 * tile, 2 * tile + 2):
            p, lane = piece * LANES // modes, piece * LANES % modes
            parts.append(ref[(p,) + lead + (rows, slice(lane, lane + LANES))])
        return jnp.concatenate(parts, axis=1)

    tiles = species * modes // width
    units = [(k, n) for k in range(block) for n in range(everyone // width)]
    pending = []

    def drain():
        while pending:
            acc, k, n = pending.pop(0)
            columns = slice(n * width, (n + 1) * width)
            inner = pltpu.matmul_pop(acc)
            row = jnp.sum(inner * own[:, columns], axis=0, keepdims=True)
            total[pl.ds(step * block + k, 1), columns] = row

    def multiply(*sums):
        for at in range(0, len(units), 2):
            pair = units[at : at + 2]

            def push(tile):
                for unit, (k, n) in enumerate(pair):
                    rows = slice(n * width, (n + 1) * width)
                    pltpu.matmul_push_rhs(strip(other, (), rows, tile), tile % 2, unit, transpose=True)

            push(0)
            for tile in range(tiles):
                if tile + 1 < tiles:
                    push(tile + 1)
                for unit, (k, n) in enumerate(pair):
                    acc = sums[2 * unit + (at // 2) % 2]
                    pltpu.matmul_acc_lhs(acc, strip(tensors, (k,), slice(None), tile), tile % 2)
                if tile == 0:
                    drain()
            for unit, (k, n) in enumerate(pair):
                pending.append((sums[2 * unit + (at // 2) % 2], k, n))
        drain()

    pl.run_scoped(
        multiply, *[pltpu.ACC(unit)((modes, width), jnp.float32) for unit in (0, 0, 1, 1)]
    )

    @pl.when(step == pl.num_programs(0) - 1)
    def _():
        here = lax.axis_index("cell")
        whole = total[...].T
        out_modes = whole.shape[1]
        fold = fold_of(cells, out_modes)
        rows = cells // fold
        flag = limiter[:, cells - 1 :].astype(jnp.float32)
        spare = jnp.broadcast_to(flag, (rows, LANES - fold * out_modes))
        for d in range(groups):
            first = d * cells
            parts = [whole[first + f * rows : first + (f + 1) * rows] for f in range(fold)]
            out[lax.rem(here + groups - d, groups)] = jnp.concatenate(parts + [spare], axis=1)


def collide(table, spread, tensors, limiter):
    species = len(spread)
    groups, cells, modes = spread[0].shape
    out_modes = tensors.shape[1]
    rows = cells // fold_of(cells, out_modes)
    block = max(b for b in (1, 2, 4, 6, 8) if out_modes % b == 0)
    vmem = pl.BlockSpec(memory_space=pltpu.VMEM)
    return pl.pallas_call(
        functools.partial(collide_kernel, species=species),
        grid=(out_modes // block,),
        in_specs=[
            pl.BlockSpec(memory_space=pltpu.SMEM),
            *[vmem] * species,
            pl.BlockSpec((species, block, modes, modes), lambda step: (0, step, 0, 0)),
            vmem,
        ],
        out_specs=vmem,
        scratch_shapes=[
            pltpu.VMEM((species, groups * cells, modes), jnp.bfloat16),
            pltpu.VMEM((modes, groups * cells), jnp.float32),
            pltpu.VMEM((out_modes, groups * cells), jnp.float32),
        ],
        out_shape=jax.ShapeDtypeStruct((groups, rows, LANES), jnp.float32),
        compiler_params=pltpu.CompilerParams(vmem_limit_bytes=40 * MIB),
        name="collide",
    )(table, *spread, tensors, limiter)


def flux_kernel(mine, limiter, plus, minus, flux):
    groups, cells, modes = mine.shape
    wide = jnp.concatenate([mine[d].astype(jnp.float32) for d in (1, 0, groups - 1)], axis=0)
    wide = wide[cells - 2 : 2 * cells + 2]
    lower = wide[1:-1] - wide[:-2]
    upper = wide[2:] - wide[1:-1]
    one = minmod_two(lower, upper)
    two = minmod_three(2.0 * lower, 0.5 * (lower + upper), 2.0 * upper)
    flags = column(limiter[...])
    ahead = lax.broadcasted_iota(jnp.int32, (3, 1), 0)

    def chosen(first, second, flag):
        return jnp.where(flag == 1, first, jnp.where(flag == 2, second, 0.0))

    def stack(shift):
        base = wide[1 + shift :]
        faces = base[1 : cells + 1]
        faces = faces + (0.5 - shift) * chosen(
            one[1 + shift : 1 + shift + cells], two[1 + shift : 1 + shift + cells], flags
        )
        edge = base[:1] + (0.5 - shift) * chosen(
            one[shift : shift + 1], two[shift : shift + 1], ahead
        )
        pad = jnp.zeros((flux.shape[0] - cells - 3, modes), jnp.float32)
        return jnp.concatenate([faces, edge, pad], axis=0)

    total = jnp.dot(
        stack(0), plus[0], precision=lax.Precision.HIGHEST, preferred_element_type=jnp.float32
    )
    total = total + jnp.dot(
        stack(1), minus[0], precision=lax.Precision.HIGHEST, preferred_element_type=jnp.float32
    )
    flux[...] = total


def transport(mine, limiter, plus, minus):
    groups, cells, modes = mine.shape
    vmem = pl.BlockSpec(memory_space=pltpu.VMEM)
    return pl.pallas_call(
        flux_kernel,
        in_specs=[vmem, vmem, vmem, vmem],
        out_specs=vmem,
        out_shape=jax.ShapeDtypeStruct((cells + 8, modes), jnp.float32),
        compiler_params=pltpu.CompilerParams(vmem_limit_bytes=16 * MIB),
        name="transport",
    )(mine, limiter, plus, minus)


def finish_kernel(out_modes, received, flux, fields, new_field, collision):
    groups, rows, _ = received.shape
    cells = fields.shape[1]
    fold = cells // rows
    parts = []
    for f in range(fold):
        pieces = [received[g][:, f * out_modes : (f + 1) * out_modes] for g in range(groups)]
        parts.append(jnp.concatenate(pieces, axis=1))
    term = jnp.concatenate(parts, axis=0)
    collision[0] = term
    before = lax.rem(lax.axis_index("cell") + groups - 1, groups)
    flag = received[before][:1, fold * out_modes : fold * out_modes + 1]
    behind = flux[cells : cells + 3]
    edge = jnp.where(flag == 1.0, behind[1:2], jnp.where(flag == 2.0, behind[2:3], behind[:1]))
    faces = flux[:cells]
    ahead = jnp.concatenate([edge, faces[:-1]], axis=0)
    new_field[0] = fields[0].astype(jnp.float32) + 0.4 * (ahead - faces) + 0.5 * term


def finish(received, flux, fields, out_modes):
    vmem = pl.BlockSpec(memory_space=pltpu.VMEM)
    shape = jax.ShapeDtypeStruct(fields.shape, jnp.float32)
    return pl.pallas_call(
        functools.partial(finish_kernel, out_modes),
        in_specs=[vmem, vmem, vmem],
        out_specs=(vmem, vmem),
        out_shape=(shape, shape),
        compiler_params=pltpu.CompilerParams(vmem_limit_bytes=16 * MIB),
        name="finish",
    )(received, flux, fields)


def shifted(x, axis, by):
    size = lax.axis_size(axis)
    return lax.ppermute(x, axis, [(i, (i + by) % size) for i in range(size)])


def exchanged(x, axis, bit):
    return lax.ppermute(x, axis, [(i, i ^ bit) for i in range(lax.axis_size(axis))])


def local(fields, tensors, pair_table, plus_flux, minus_flux, face_limiter):
    groups, species = lax.axis_size("cell"), lax.axis_size("spec")
    mine = jnp.stack([fields[0]] + [shifted(fields[0], "cell", d) for d in range(1, groups)])
    spread = {0: mine}
    bit = species // 2
    while bit > 0:
        spread.update({q | bit: exchanged(x, "spec", bit) for q, x in spread.items()})
        bit //= 2
    spread = [spread[q] for q in range(species)]
    block = collide(pair_table, spread, tensors, face_limiter)
    received = lax.all_to_all(block, "cell", split_axis=0, concat_axis=0, tiled=False)
    flux = transport(mine, face_limiter, plus_flux, minus_flux)
    return finish(received, flux, fields, tensors.shape[1])


def solution(mesh):
    placed = (
        P("spec", "cell", None),
        P("spec", "cell", None, None),
        P(),
        P("spec", None, None),
        P("spec", None, None),
        P("spec", "cell"),
    )
    return jax.shard_map(
        local,
        mesh=mesh,
        in_specs=placed,
        out_specs=(P("spec", "cell", None), P("spec", "cell", None)),
        check_vma=False,
    )
```

```python
import functools

import jax
import jax.numpy as jnp
from jax import lax
from jax.experimental import pallas as pl
from jax.experimental.pallas import tpu as pltpu
from jax.sharding import PartitionSpec as P

LANES = 128
MIB = 1 << 20
WORK = 3 * MIB
PARTS = 4


def minmod_two(first, second):
    least = jnp.minimum(jnp.abs(first), jnp.abs(second))
    return jnp.where(first * second > 0, jnp.where(first > 0, least, -least), 0.0)


def minmod_three(first, second, third):
    same = (first * second > 0) & (second * third > 0)
    least = jnp.minimum(jnp.minimum(jnp.abs(first), jnp.abs(second)), jnp.abs(third))
    return jnp.where(same, jnp.where(first > 0, least, -least), 0.0)


def column(row):
    n = row.shape[1]
    down = lax.broadcasted_iota(jnp.int32, (n, n), 0)
    across = lax.broadcasted_iota(jnp.int32, (n, n), 1)
    return jnp.sum(jnp.where(down == across, row, 0), axis=1, keepdims=True)


def fold_of(cells, out_modes):
    fold = 1
    while cells % (2 * fold) == 0 and 2 * fold * out_modes < LANES:
        fold *= 2
    return fold


def reverse(number, count):
    out, bit = 0, 1
    while bit < count:
        out = out * 2 + number // bit % 2
        bit *= 2
    return out


def slot_of(here, there, groups):
    difference = here ^ there
    out, bit = 0, 0
    while (1 << bit) < groups:
        out = out * 2 + ((difference >> bit) & 1)
        bit += 1
    return out


def tensor_of(table, species, partner):
    owner = lax.axis_index("spec")
    return table[owner, owner ^ partner] - owner * species


def fetches(table, tensors, near, sems, first, partners, pieces):
    count = near.shape[1] // pieces
    copies = []
    for at, partner in enumerate(partners):
        p = tensor_of(table, tensors.shape[0], partner)
        for piece in range(pieces):
            copies.append(
                pltpu.make_async_copy(
                    tensors.at[p, pl.ds(first + piece * count, count)],
                    near.at[at, pl.ds(piece * count, count)],
                    sems.at[at * pieces + piece],
                )
            )
    return copies


def close(x):
    return pltpu.with_memory_space_constraint(x, pltpu.VMEM)


def fetch_kernel(table, after, tensors, near, token, sems, *, first, partners, pieces):
    copies = fetches(table, tensors, near, sems, first, partners, pieces)
    for copy in copies:
        copy.start()
    token[...] = jnp.zeros_like(token)
    for copy in copies:
        copy.wait()


def fetch(table, after, tensors, first, count, partners):
    pieces = max(d for d in (1, 2, 3, 4) if count % d == 0)
    shape = (len(partners), count) + tensors.shape[2:]
    anywhere = pl.BlockSpec(memory_space=pl.ANY)
    vmem = pl.BlockSpec(memory_space=pltpu.VMEM)
    return pl.pallas_call(
        functools.partial(fetch_kernel, first=first, partners=partners, pieces=pieces),
        in_specs=[pl.BlockSpec(memory_space=pltpu.SMEM), anywhere, anywhere],
        out_specs=(vmem, vmem),
        scratch_shapes=[pltpu.SemaphoreType.DMA((len(partners) * pieces,))],
        out_shape=(pltpu.VMEM(shape, tensors.dtype), pltpu.VMEM((8, LANES), jnp.float32)),
        compiler_params=pltpu.CompilerParams(vmem_limit_bytes=MIB),
        cost_estimate=pl.CostEstimate(
            flops=0, transcendentals=0, bytes_accessed=2 * shape[0] * count * shape[2] * shape[3]
        ),
        name="fetch",
    )(table, after, tensors)


def contract(parts, other, own, total, add):
    partners, groups, cells, modes = other.shape
    everyone = groups * cells
    width = 2 * LANES
    tiles = partners * modes // width
    spans = everyone // width

    def unit_of(pair, unit):
        at = 2 * pair + unit
        if spans == 1:
            return at, 0
        return at // spans, at % spans

    def columns_of(span):
        return slice(0, width) if spans == 1 else pl.ds(pl.multiple_of(span * width, width), width)

    def pieces_of(tile):
        for piece in (2 * tile, 2 * tile + 1):
            yield piece * LANES // modes, slice(piece * LANES % modes, piece * LANES % modes + LANES)

    def push(pair, tile, register):
        for unit in range(2):
            _, span = unit_of(pair, unit)
            of = width // cells
            rows = slice(0, of) if spans == 1 else pl.ds(span * of, of)
            tall = [other[p, rows, :, lanes].reshape(width, LANES) for p, lanes in pieces_of(tile)]
            pltpu.matmul_push_rhs(jnp.concatenate(tall, axis=1), register, unit, transpose=True)

    def run(*sums):
        def drain(offset, pair, bank):
            for unit in range(2):
                k, span = unit_of(pair, unit)
                columns = columns_of(span)
                inner = pltpu.matmul_pop(sums[2 * unit + bank])
                row = jnp.sum(inner * own[:, columns], axis=0, keepdims=True)
                place = pl.ds(offset + k, 1)
                total[place, columns] = row + add[place, columns] if add is not None else row

        def work(part, pair, bank, start, follower, pending):
            for tile in range(tiles):
                register = (start + tile) % 2
                if tile + 1 < tiles:
                    push(pair, tile + 1, 1 - register)
                elif follower is not None:
                    push(follower, 0, 1 - register)
                for unit in range(2):
                    k, _ = unit_of(pair, unit)
                    wide = [part[p, k, :, lanes] for p, lanes in pieces_of(tile)]
                    pltpu.matmul_acc_lhs(
                        sums[2 * unit + bank], jnp.concatenate(wide, axis=1), register
                    )
                if tile == 0 and pending is not None:
                    drain(*pending)
            return (start + tiles) % 2

        offset, pending, at = 0, None, 0
        push(0, 0, at)
        for number, part in enumerate(parts):
            pairs = part.shape[1] * spans // 2
            at = work(part, 0, 0, at, 1, pending)
            odd = at

            @pl.loop(0, (pairs - 2) // 2)
            def _(step):
                now = work(part, 2 * step + 1, 1, odd, 2 * step + 2, (offset, 2 * step, 0))
                work(part, 2 * step + 2, 0, now, 2 * step + 3, (offset, 2 * step + 1, 1))

            last = number + 1 == len(parts)
            at = work(part, pairs - 1, 1, odd, None if last else 0, (offset, pairs - 2, 0))
            pending = (offset, pairs - 1, 1)
            offset += part.shape[1]
        drain(*pending)

    pl.run_scoped(run, *[pltpu.ACC(unit)((modes, width), jnp.float32) for unit in (0, 0, 1, 1)])


def near_kernel(table, mine, mate, tensors, *refs, partners, pieces):
    parts, (total, own, far, other, sems, load) = refs[:PARTS], refs[PARTS:]
    copies = fetches(table, tensors, far, sems, 0, partners, pieces)
    loads = [pltpu.make_async_copy(x, other.at[at], load.at[at]) for at, x in enumerate((mine, mate))]
    for copy in loads + copies:
        copy.start()
    for copy in loads:
        copy.wait()
    own[...] = other[0].reshape(own.shape[::-1]).astype(jnp.float32).T
    contract(parts, other, own, total, None)
    for copy in copies:
        copy.wait()


def collide_near(table, mine, mate, tensors, parts, partners):
    groups, cells, modes = mine.shape
    out_modes = tensors.shape[1]
    pieces = max(d for d in (1, 2, 3, 4, 6, 8) if out_modes % d == 0)
    anywhere = pl.BlockSpec(memory_space=pl.ANY)
    vmem = pl.BlockSpec(memory_space=pltpu.VMEM)
    return pl.pallas_call(
        functools.partial(near_kernel, partners=partners, pieces=pieces),
        in_specs=[pl.BlockSpec(memory_space=pltpu.SMEM), anywhere, anywhere, anywhere]
        + [vmem] * len(parts),
        out_specs=(vmem, vmem, vmem),
        scratch_shapes=[
            pltpu.VMEM((2, groups, cells, modes), jnp.bfloat16),
            pltpu.SemaphoreType.DMA((len(partners) * pieces,)),
            pltpu.SemaphoreType.DMA((2,)),
        ],
        out_shape=(
            pltpu.VMEM((out_modes, groups * cells), jnp.float32),
            pltpu.VMEM((modes, groups * cells), jnp.float32),
            pltpu.VMEM((len(partners),) + tensors.shape[1:], tensors.dtype),
        ),
        compiler_params=pltpu.CompilerParams(vmem_limit_bytes=WORK),
        cost_estimate=pl.CostEstimate(
            flops=2 * tensors.size // 2 * groups * cells,
            transcendentals=0,
            bytes_accessed=tensors.size,
        ),
        name="collide_near",
    )(table, mine, mate, tensors, *[close(part) for part in parts])


def far_kernel(one, two, far, first, own, limiter, keep, send, other, total, load):
    loads = [pltpu.make_async_copy(x, other.at[at], load.at[at]) for at, x in enumerate((one, two))]
    for copy in loads:
        copy.start()
    for copy in loads:
        copy.wait()
    contract((far,), other, own, total, first)
    _, groups, cells, _ = other.shape
    whole = total[...].T
    out_modes = whole.shape[1]
    fold = fold_of(cells, out_modes)
    rows = cells // fold
    flag = limiter[:, cells - 1 :].astype(jnp.float32)
    spare = jnp.broadcast_to(flag, (rows, LANES - fold * out_modes))
    for d in range(groups):
        start = d * cells
        parts = [whole[start + f * rows : start + (f + 1) * rows] for f in range(fold)]
        block = jnp.concatenate(parts + [spare], axis=1)
        slot = reverse(d, groups)
        half = groups // 2
        if slot < half:
            keep[slot] = block
        else:
            send[slot - half] = block


def collide_far(one, two, far, first, own, limiter):
    groups, cells, modes = one.shape
    out_modes = far.shape[1]
    rows = cells // fold_of(cells, out_modes)
    anywhere = pl.BlockSpec(memory_space=pl.ANY)
    vmem = pl.BlockSpec(memory_space=pltpu.VMEM)
    half = pltpu.VMEM((groups // 2, rows, LANES), jnp.float32)
    return pl.pallas_call(
        far_kernel,
        in_specs=[anywhere, anywhere, vmem, vmem, vmem, vmem],
        out_specs=(vmem, vmem),
        scratch_shapes=[
            pltpu.VMEM((2, groups, cells, modes), jnp.bfloat16),
            pltpu.VMEM((out_modes, groups * cells), jnp.float32),
            pltpu.SemaphoreType.DMA((2,)),
        ],
        out_shape=(half, half),
        compiler_params=pltpu.CompilerParams(vmem_limit_bytes=WORK),
        cost_estimate=pl.CostEstimate(
            flops=2 * far.size * groups * cells, transcendentals=0, bytes_accessed=far.size
        ),
        name="collide_far",
    )(one, two, close(far), close(first), close(own), limiter)


def flux_kernel(mine, limiter, plus, minus, flux):
    groups, cells, modes = mine.shape
    place = lax.axis_index("cell")
    before = slot_of(place, lax.rem(place + groups - 1, groups), groups)
    after = slot_of(place, lax.rem(place + 1, groups), groups)
    wide = jnp.concatenate([mine[d].astype(jnp.float32) for d in (before, 0, after)], axis=0)
    wide = wide[cells - 2 : 2 * cells + 2]
    lower = wide[1:-1] - wide[:-2]
    upper = wide[2:] - wide[1:-1]
    one = minmod_two(lower, upper)
    two = minmod_three(2.0 * lower, 0.5 * (lower + upper), 2.0 * upper)
    flags = column(limiter[...])
    ahead = lax.broadcasted_iota(jnp.int32, (3, 1), 0)

    def chosen(first, second, flag):
        return jnp.where(flag == 1, first, jnp.where(flag == 2, second, 0.0))

    def stack(shift):
        base = wide[1 + shift :]
        faces = base[1 : cells + 1]
        faces = faces + (0.5 - shift) * chosen(
            one[1 + shift : 1 + shift + cells], two[1 + shift : 1 + shift + cells], flags
        )
        edge = base[:1] + (0.5 - shift) * chosen(
            one[shift : shift + 1], two[shift : shift + 1], ahead
        )
        pad = jnp.zeros((flux.shape[0] - cells - 3, modes), jnp.float32)
        return jnp.concatenate([faces, edge, pad], axis=0)

    total = jnp.dot(
        stack(0), plus[0], precision=lax.Precision.HIGHEST, preferred_element_type=jnp.float32
    )
    total = total + jnp.dot(
        stack(1), minus[0], precision=lax.Precision.HIGHEST, preferred_element_type=jnp.float32
    )
    flux[...] = total


def transport(mine, limiter, plus, minus):
    groups, cells, modes = mine.shape
    vmem = pl.BlockSpec(memory_space=pltpu.VMEM)
    return pl.pallas_call(
        flux_kernel,
        in_specs=[vmem, vmem, vmem, vmem],
        out_specs=vmem,
        out_shape=jax.ShapeDtypeStruct((cells + 8, modes), jnp.float32),
        compiler_params=pltpu.CompilerParams(vmem_limit_bytes=4 * MIB),
        name="transport",
    )(mine, limiter, plus, minus)


def finish_kernel(out_modes, received, flux, fields, new_field, collision):
    groups, rows, _ = received.shape
    place = lax.axis_index("cell")
    blocks = [received[slot_of(place, g, groups)] for g in range(groups)]
    cells = fields.shape[1]
    fold = cells // rows
    parts = []
    for f in range(fold):
        pieces = [blocks[g][:, f * out_modes : (f + 1) * out_modes] for g in range(groups)]
        parts.append(jnp.concatenate(pieces, axis=1))
    term = jnp.concatenate(parts, axis=0)
    collision[0] = term
    before = slot_of(place, lax.rem(place + groups - 1, groups), groups)
    flag = received[before][:1, fold * out_modes : fold * out_modes + 1]
    behind = flux[cells : cells + 3]
    edge = jnp.where(flag == 1.0, behind[1:2], jnp.where(flag == 2.0, behind[2:3], behind[:1]))
    faces = flux[:cells]
    ahead = jnp.concatenate([edge, faces[:-1]], axis=0)
    new_field[0] = fields[0].astype(jnp.float32) + 0.4 * (ahead - faces) + 0.5 * term


def finish(received, flux, fields, out_modes):
    vmem = pl.BlockSpec(memory_space=pltpu.VMEM)
    shape = jax.ShapeDtypeStruct(fields.shape, jnp.float32)
    return pl.pallas_call(
        functools.partial(finish_kernel, out_modes),
        in_specs=[vmem, vmem, vmem],
        out_specs=(vmem, vmem),
        out_shape=(shape, shape),
        compiler_params=pltpu.CompilerParams(vmem_limit_bytes=4 * MIB),
        name="finish",
    )(received, flux, fields)


def exchanged(x, axis, bit):
    return lax.ppermute(x, axis, [(i, i ^ bit) for i in range(lax.axis_size(axis))])


def ordered(x, token):
    return lax.optimization_barrier((x, token))[0]


def local(fields, tensors, pair_table, plus_flux, minus_flux, face_limiter):
    groups, species = lax.axis_size("cell"), lax.axis_size("spec")
    count = tensors.shape[1] // PARTS
    mine = fields
    parts = []
    token = fields
    bit = groups // 2
    while bit > 0:
        came = exchanged(mine, "cell", bit)
        if len(parts) < PARTS - 1:
            part, token = fetch(pair_table, mine, tensors, len(parts) * count, count, (0, 1))
            parts.append(part)
            came = ordered(came, token)
        mine = jnp.concatenate([mine, came], axis=0)
        bit //= 2
    mate = exchanged(mine, "spec", 1)
    far_one = exchanged(mine, "spec", 2)
    while len(parts) < PARTS:
        part, token = fetch(pair_table, mine, tensors, len(parts) * count, count, (0, 1))
        parts.append(part)
    mate = ordered(mate, token)
    far_two = exchanged(mate, "spec", 2)
    first, own, far = collide_near(pair_table, mine, mate, tensors, parts, (2, 3))
    keep, send = collide_far(far_one, far_two, far, first, own, face_limiter)
    flux = transport(mine, face_limiter, plus_flux, minus_flux)
    keep, send = keep[None], send[None]
    bit = groups // 2
    while True:
        keep = jnp.concatenate([keep, exchanged(send, "cell", bit)], axis=0)
        bit //= 2
        if bit == 0:
            break
        keep, send = keep[:, :bit], keep[:, bit:]
    return finish(keep[:, 0], flux, fields, tensors.shape[1])


def solution(mesh):
    placed = (
        P("spec", "cell", None),
        P("spec", "cell", None, None),
        P(),
        P("spec", None, None),
        P("spec", None, None),
        P("spec", "cell"),
    )
    return jax.shard_map(
        local,
        mesh=mesh,
        in_specs=placed,
        out_specs=(P("spec", "cell", None), P("spec", "cell", None)),
        check_vma=False,
    )
```

```python
import functools

import jax
import jax.numpy as jnp
from jax import lax
from jax.experimental import pallas as pl
from jax.experimental.pallas import tpu as pltpu
from jax.sharding import PartitionSpec as P

LANES = 128
MIB = 1 << 20
PARTS = 4


def minmod_two(first, second):
    least = jnp.minimum(jnp.abs(first), jnp.abs(second))
    return jnp.where(first * second > 0, jnp.where(first > 0, least, -least), 0.0)


def minmod_three(first, second, third):
    same = (first * second > 0) & (second * third > 0)
    least = jnp.minimum(jnp.minimum(jnp.abs(first), jnp.abs(second)), jnp.abs(third))
    return jnp.where(same, jnp.where(first > 0, least, -least), 0.0)


def column(row):
    n = row.shape[1]
    down = lax.broadcasted_iota(jnp.int32, (n, n), 0)
    across = lax.broadcasted_iota(jnp.int32, (n, n), 1)
    return jnp.sum(jnp.where(down == across, row, 0), axis=1, keepdims=True)


def fold_of(cells, out_modes):
    fold = 1
    while cells % (2 * fold) == 0 and 2 * fold * out_modes < LANES:
        fold *= 2
    return fold


def close(x):
    return pltpu.with_memory_space_constraint(x, pltpu.VMEM)


def tensor_of(table, partner):
    owner = lax.axis_index("spec")
    return table[owner, owner ^ partner] - owner * table.shape[0]


def fetch_kernel(table, tensors, near, token, sem):
    copy = pltpu.make_async_copy(tensors.at[tensor_of(table, 0)], near, sem)
    copy.start()
    token[...] = jnp.zeros_like(token)
    copy.wait()


def fetch(table, tensors):
    shape = tensors.shape[1:]
    vmem = pl.BlockSpec(memory_space=pltpu.VMEM)
    return pl.pallas_call(
        fetch_kernel,
        in_specs=[pl.BlockSpec(memory_space=pltpu.SMEM), pl.BlockSpec(memory_space=pl.ANY)],
        out_specs=(vmem, vmem),
        scratch_shapes=[pltpu.SemaphoreType.DMA],
        out_shape=(pltpu.VMEM(shape, tensors.dtype), pltpu.VMEM((8, LANES), jnp.float32)),
        compiler_params=pltpu.CompilerParams(vmem_limit_bytes=MIB),
        cost_estimate=pl.CostEstimate(
            flops=0, transcendentals=0, bytes_accessed=4 * tensors.size // tensors.shape[0]
        ),
        name="fetch",
    )(table, tensors)


def contract(read, count, others, own, total, add, ahead):
    groups, cells, modes = others[0].shape
    everyone = groups * cells
    width = 2 * LANES
    tiles = len(others) * modes // width
    spans = everyone // width
    pairs = count * spans // 2

    def unit_of(pair, unit):
        at = 2 * pair + unit
        if spans == 1:
            return at, 0
        return at // spans, at % spans

    def columns_of(span):
        return slice(0, width) if spans == 1 else pl.ds(pl.multiple_of(span * width, width), width)

    def pieces_of(tile):
        for piece in (2 * tile, 2 * tile + 1):
            yield piece * LANES // modes, slice(piece * LANES % modes, piece * LANES % modes + LANES)

    def push(pair, tile, register):
        for unit in range(2):
            _, span = unit_of(pair, unit)
            of = width // cells
            rows = slice(0, of) if spans == 1 else pl.ds(span * of, of)
            tall = [others[p][rows, :, lanes].reshape(width, LANES) for p, lanes in pieces_of(tile)]
            pltpu.matmul_push_rhs(jnp.concatenate(tall, axis=1), register, unit, transpose=True)

    def run(*sums):
        def drain(part, pair, bank):
            for unit in range(2):
                k, span = unit_of(pair, unit)
                columns = columns_of(span)
                inner = pltpu.matmul_pop(sums[2 * unit + bank])
                row = jnp.sum(inner * own[:, columns], axis=0, keepdims=True)
                place = pl.ds(part * count + k, 1)
                total[place, columns] = row + add[place, columns] if add is not None else row

        def work(part, pair, bank, start, follower, pending):
            for tile in range(tiles):
                register = (start + tile) % 2
                if tile + 1 < tiles:
                    push(pair, tile + 1, 1 - register)
                elif follower is not None:
                    push(follower, 0, 1 - register)
                for unit in range(2):
                    k, _ = unit_of(pair, unit)
                    wide = [read(p, part, k, lanes) for p, lanes in pieces_of(tile)]
                    pltpu.matmul_acc_lhs(
                        sums[2 * unit + bank], jnp.concatenate(wide, axis=1), register
                    )
                if tile == 0 and pending is not None:
                    drain(*pending)
            return (start + tiles) % 2

        pending, at = None, 0
        push(0, 0, at)
        for part in range(PARTS):
            ahead(part)
            at = work(part, 0, 0, at, 1, pending)
            odd = at

            @pl.loop(0, (pairs - 2) // 2)
            def _(step):
                now = work(part, 2 * step + 1, 1, odd, 2 * step + 2, (part, 2 * step, 0))
                work(part, 2 * step + 2, 0, now, 2 * step + 3, (part, 2 * step + 1, 1))

            follower = None if part + 1 == PARTS else 0
            at = work(part, pairs - 1, 1, odd, follower, (part, pairs - 2, 0))
            pending = (part, pairs - 1, 1)
        drain(*pending)

    pl.run_scoped(run, *[pltpu.ACC(unit)((modes, width), jnp.float32) for unit in (0, 0, 1, 1)])


def near_kernel(table, mine, mate, tensors, near, total, own, far, beside, sems):
    count = tensors.shape[1] // PARTS
    second = tensor_of(table, 1)
    copies = [
        pltpu.make_async_copy(
            tensors.at[second, pl.ds(part * count, count)],
            beside.at[pl.ds(part * count, count)],
            sems.at[part],
        )
        for part in range(PARTS)
    ] + [
        pltpu.make_async_copy(
            tensors.at[tensor_of(table, 2 + at), pl.ds(0, count)], far.at[at], sems.at[PARTS + at]
        )
        for at in range(2)
    ]
    copies[0].start()
    copies[1].start()
    own[...] = mine[...].reshape(own.shape[::-1]).astype(jnp.float32).T

    def ahead(part):
        copies[part].wait()
        if part + 2 < len(copies):
            copies[part + 2].start()

    def read(p, part, k, lanes):
        return (near, beside)[p][part * count + k, :, lanes]

    contract(read, count, (mine, mate), own, total, None, ahead)
    for copy in copies[PARTS:]:
        copy.wait()


def collide_near(table, mine, mate, tensors, near):
    groups, cells, modes = mine.shape
    out_modes = tensors.shape[1]
    vmem = pl.BlockSpec(memory_space=pltpu.VMEM)
    return pl.pallas_call(
        near_kernel,
        in_specs=[
            pl.BlockSpec(memory_space=pltpu.SMEM),
            vmem,
            vmem,
            pl.BlockSpec(memory_space=pl.ANY),
            vmem,
        ],
        out_specs=(vmem, vmem, vmem),
        scratch_shapes=[
            pltpu.VMEM(tensors.shape[1:], tensors.dtype),
            pltpu.SemaphoreType.DMA((PARTS + 2,)),
        ],
        out_shape=(
            pltpu.VMEM((out_modes, groups * cells), jnp.float32),
            pltpu.VMEM((modes, groups * cells), jnp.float32),
            pltpu.VMEM((2, out_modes // PARTS) + tensors.shape[2:], tensors.dtype),
        ),
        compiler_params=pltpu.CompilerParams(vmem_limit_bytes=17 * MIB),
        cost_estimate=pl.CostEstimate(
            flops=tensors.size * groups * cells, transcendentals=0, bytes_accessed=tensors.size
        ),
        name="collide_near",
    )(table, close(mine), close(mate), tensors, close(near))


def far_kernel(table, one, two, tensors, far, first, own, limiter, out, total, rest, sems):
    count = tensors.shape[1] // PARTS
    copies = [
        [
            pltpu.make_async_copy(
                tensors.at[tensor_of(table, 2 + at), pl.ds(part * count, count)],
                rest.at[at, pl.ds((part - 1) * count, count)],
                sems.at[at, part - 1],
            )
            for at in range(2)
        ]
        for part in range(1, PARTS)
    ]
    for copy in copies[0] + copies[1]:
        copy.start()

    def ahead(part):
        if part > 0:
            for copy in copies[part - 1]:
                copy.wait()
            for copy in copies[part + 1] if part + 1 < len(copies) else ():
                copy.start()

    def read(p, part, k, lanes):
        return far[p, k, :, lanes] if part == 0 else rest[p, (part - 1) * count + k, :, lanes]

    contract(read, count, (one, two), own, total, first, ahead)
    groups, cells, _ = one.shape
    whole = total[...].T
    out_modes = whole.shape[1]
    fold = fold_of(cells, out_modes)
    rows = cells // fold
    flag = limiter[:, cells - 1 :].astype(jnp.float32)
    spare = jnp.broadcast_to(flag, (rows, LANES - fold * out_modes))
    for d in range(groups):
        start = d * cells
        parts = [whole[start + f * rows : start + (f + 1) * rows] for f in range(fold)]
        out[d] = jnp.concatenate(parts + [spare], axis=1)


def collide_far(table, one, two, tensors, far, first, own, limiter):
    groups, cells, modes = one.shape
    out_modes = tensors.shape[1]
    count = out_modes // PARTS
    rows = cells // fold_of(cells, out_modes)
    vmem = pl.BlockSpec(memory_space=pltpu.VMEM)
    return pl.pallas_call(
        far_kernel,
        in_specs=[
            pl.BlockSpec(memory_space=pltpu.SMEM),
            vmem,
            vmem,
            pl.BlockSpec(memory_space=pl.ANY),
            vmem,
            vmem,
            vmem,
            vmem,
        ],
        out_specs=vmem,
        scratch_shapes=[
            pltpu.VMEM((out_modes, groups * cells), jnp.float32),
            pltpu.VMEM((2, out_modes - count) + tensors.shape[2:], tensors.dtype),
            pltpu.SemaphoreType.DMA((2, PARTS - 1)),
        ],
        out_shape=pltpu.VMEM((groups, rows, LANES), jnp.float32),
        compiler_params=pltpu.CompilerParams(vmem_limit_bytes=24 * MIB),
        cost_estimate=pl.CostEstimate(
            flops=tensors.size * groups * cells, transcendentals=0, bytes_accessed=tensors.size
        ),
        name="collide_far",
    )(table, close(one), close(two), tensors, close(far), close(first), close(own), limiter)


def flux_kernel(mine, limiter, plus, minus, flux):
    groups, cells, modes = mine.shape
    here = lax.axis_index("cell")
    around = (lax.rem(here + groups - 1, groups), here, lax.rem(here + 1, groups))
    wide = jnp.concatenate([mine[d].astype(jnp.float32) for d in around], axis=0)
    wide = wide[cells - 2 : 2 * cells + 2]
    lower = wide[1:-1] - wide[:-2]
    upper = wide[2:] - wide[1:-1]
    one = minmod_two(lower, upper)
    two = minmod_three(2.0 * lower, 0.5 * (lower + upper), 2.0 * upper)
    flags = column(limiter[...])
    ahead = lax.broadcasted_iota(jnp.int32, (3, 1), 0)

    def chosen(first, second, flag):
        return jnp.where(flag == 1, first, jnp.where(flag == 2, second, 0.0))

    def stack(shift):
        base = wide[1 + shift :]
        faces = base[1 : cells + 1]
        faces = faces + (0.5 - shift) * chosen(
            one[1 + shift : 1 + shift + cells], two[1 + shift : 1 + shift + cells], flags
        )
        edge = base[:1] + (0.5 - shift) * chosen(
            one[shift : shift + 1], two[shift : shift + 1], ahead
        )
        pad = jnp.zeros((flux.shape[0] - cells - 3, modes), jnp.float32)
        return jnp.concatenate([faces, edge, pad], axis=0)

    total = jnp.dot(
        stack(0), plus[0], precision=lax.Precision.HIGHEST, preferred_element_type=jnp.float32
    )
    total = total + jnp.dot(
        stack(1), minus[0], precision=lax.Precision.HIGHEST, preferred_element_type=jnp.float32
    )
    flux[...] = total


def transport(mine, limiter, plus, minus):
    groups, cells, modes = mine.shape
    vmem = pl.BlockSpec(memory_space=pltpu.VMEM)
    return pl.pallas_call(
        flux_kernel,
        in_specs=[vmem, vmem, vmem, vmem],
        out_specs=vmem,
        out_shape=jax.ShapeDtypeStruct((cells + 8, modes), jnp.float32),
        compiler_params=pltpu.CompilerParams(vmem_limit_bytes=4 * MIB),
        name="transport",
    )(close(mine), limiter, plus, minus)


def finish_kernel(out_modes, received, flux, fields, new_field, collision):
    groups, rows, _ = received.shape
    cells = fields.shape[1]
    fold = cells // rows
    parts = []
    for f in range(fold):
        pieces = [received[g][:, f * out_modes : (f + 1) * out_modes] for g in range(groups)]
        parts.append(jnp.concatenate(pieces, axis=1))
    term = jnp.concatenate(parts, axis=0)
    collision[0] = term
    before = lax.rem(lax.axis_index("cell") + groups - 1, groups)
    flag = received[before][:1, fold * out_modes : fold * out_modes + 1]
    behind = flux[cells : cells + 3]
    edge = jnp.where(flag == 1.0, behind[1:2], jnp.where(flag == 2.0, behind[2:3], behind[:1]))
    faces = flux[:cells]
    ahead = jnp.concatenate([edge, faces[:-1]], axis=0)
    new_field[0] = fields[0].astype(jnp.float32) + 0.4 * (ahead - faces) + 0.5 * term


def finish(received, flux, fields, out_modes):
    vmem = pl.BlockSpec(memory_space=pltpu.VMEM)
    shape = jax.ShapeDtypeStruct(fields.shape, jnp.float32)
    return pl.pallas_call(
        functools.partial(finish_kernel, out_modes),
        in_specs=[vmem, vmem, vmem],
        out_specs=(vmem, vmem),
        out_shape=(shape, shape),
        compiler_params=pltpu.CompilerParams(vmem_limit_bytes=4 * MIB),
        name="finish",
    )(received, flux, fields)


def exchanged(x, axis, bit):
    return lax.ppermute(x, axis, [(i, i ^ bit) for i in range(lax.axis_size(axis))])


def local(fields, tensors, pair_table, plus_flux, minus_flux, face_limiter):
    mine = lax.all_gather(fields[0], "cell", axis=0, tiled=False)
    mate = exchanged(mine, "spec", 1)
    far_one = exchanged(mine, "spec", 2)
    near, token = fetch(pair_table, tensors)
    mate = lax.optimization_barrier((mate, token))[0]
    far_two = exchanged(mate, "spec", 2)
    first, own, far = collide_near(pair_table, mine, mate, tensors, near)
    block = collide_far(pair_table, far_one, far_two, tensors, far, first, own, face_limiter)
    received = lax.all_to_all(block, "cell", split_axis=0, concat_axis=0, tiled=False)
    flux = transport(mine, face_limiter, plus_flux, minus_flux)
    return finish(received, flux, fields, tensors.shape[1])


def solution(mesh):
    placed = (
        P("spec", "cell", None),
        P("spec", "cell", None, None),
        P(),
        P("spec", None, None),
        P("spec", None, None),
        P("spec", "cell"),
    )
    return jax.shard_map(
        local,
        mesh=mesh,
        in_specs=placed,
        out_specs=(P("spec", "cell", None), P("spec", "cell", None)),
        check_vma=False,
    )
```

```python
import functools

import jax
import jax.numpy as jnp
from jax import lax
from jax.experimental import pallas as pl
from jax.experimental.pallas import tpu as pltpu
from jax.sharding import PartitionSpec as P

LANES = 128
MIB = 1 << 20
PARTS = 3


def minmod_two(first, second):
    least = jnp.minimum(jnp.abs(first), jnp.abs(second))
    return jnp.where(first * second > 0, jnp.where(first > 0, least, -least), 0.0)


def minmod_three(first, second, third):
    same = (first * second > 0) & (second * third > 0)
    least = jnp.minimum(jnp.minimum(jnp.abs(first), jnp.abs(second)), jnp.abs(third))
    return jnp.where(same, jnp.where(first > 0, least, -least), 0.0)


def column(row):
    n = row.shape[1]
    down = lax.broadcasted_iota(jnp.int32, (n, n), 0)
    across = lax.broadcasted_iota(jnp.int32, (n, n), 1)
    return jnp.sum(jnp.where(down == across, row, 0), axis=1, keepdims=True)


def fold_of(cells, out_modes):
    fold = 1
    while cells % (2 * fold) == 0 and 2 * fold * out_modes < LANES:
        fold *= 2
    return fold


def reverse(number, count):
    out, bit = 0, 1
    while bit < count:
        out = out * 2 + number // bit % 2
        bit *= 2
    return out


def slot_of(here, there, groups):
    difference = here ^ there
    out, bit = 0, 0
    while (1 << bit) < groups:
        out = out * 2 + ((difference >> bit) & 1)
        bit += 1
    return out


def close(x):
    return pltpu.with_memory_space_constraint(x, pltpu.VMEM)


def tensor_of(table, partner):
    owner = lax.axis_index("spec")
    return table[owner, owner ^ partner] - owner * table.shape[0]


def fetch_kernel(table, after, tensors, near, token, sems, *, first):
    count = near.shape[1]
    copies = [
        pltpu.make_async_copy(
            tensors.at[tensor_of(table, at), pl.ds(first, count)], near.at[at], sems.at[at]
        )
        for at in range(2)
    ]
    for copy in copies:
        copy.start()
    token[...] = jnp.zeros_like(token)
    for copy in copies:
        copy.wait()


def fetch(table, after, tensors, first, count):
    shape = (2, count) + tensors.shape[2:]
    anywhere = pl.BlockSpec(memory_space=pl.ANY)
    vmem = pl.BlockSpec(memory_space=pltpu.VMEM)
    return pl.pallas_call(
        functools.partial(fetch_kernel, first=first),
        in_specs=[pl.BlockSpec(memory_space=pltpu.SMEM), vmem, anywhere],
        out_specs=(vmem, vmem),
        scratch_shapes=[pltpu.SemaphoreType.DMA((2,))],
        out_shape=(pltpu.VMEM(shape, tensors.dtype), pltpu.VMEM((8, LANES), jnp.float32)),
        compiler_params=pltpu.CompilerParams(vmem_limit_bytes=MIB),
        cost_estimate=pl.CostEstimate(
            flops=0,
            transcendentals=0,
            bytes_accessed=4 * 2 * count * tensors.shape[2] * tensors.shape[3],
        ),
        name="fetch",
    )(table, close(after), tensors)


def join_kernel(here, came, token, out):
    count = here.shape[0]
    out[:count] = here[...]
    out[count:] = came[...]


def join(here, came, token):
    vmem = pl.BlockSpec(memory_space=pltpu.VMEM)
    return pl.pallas_call(
        join_kernel,
        in_specs=[vmem, vmem, vmem],
        out_specs=vmem,
        out_shape=pltpu.VMEM((2 * here.shape[0],) + here.shape[1:], here.dtype),
        compiler_params=pltpu.CompilerParams(vmem_limit_bytes=MIB),
        name="join",
    )(close(here), close(came), close(token))


def contract(read, count, others, own, total, add, ahead):
    groups, cells, modes = others[0].shape
    everyone = groups * cells
    width = 2 * LANES
    tiles = len(others) * modes // width
    spans = everyone // width
    pairs = count * spans // 2

    def unit_of(pair, unit):
        at = 2 * pair + unit
        if spans == 1:
            return at, 0
        return at // spans, at % spans

    def columns_of(span):
        return slice(0, width) if spans == 1 else pl.ds(pl.multiple_of(span * width, width), width)

    def pieces_of(tile):
        for piece in (2 * tile, 2 * tile + 1):
            yield piece * LANES // modes, slice(piece * LANES % modes, piece * LANES % modes + LANES)

    def push(pair, tile, register):
        for unit in range(2):
            _, span = unit_of(pair, unit)
            of = width // cells
            rows = slice(0, of) if spans == 1 else pl.ds(span * of, of)
            tall = [others[p][rows, :, lanes].reshape(width, LANES) for p, lanes in pieces_of(tile)]
            pltpu.matmul_push_rhs(jnp.concatenate(tall, axis=1), register, unit, transpose=True)

    def run(*sums):
        def drain(part, pair, bank):
            for unit in range(2):
                k, span = unit_of(pair, unit)
                columns = columns_of(span)
                inner = pltpu.matmul_pop(sums[2 * unit + bank])
                row = jnp.sum(inner * own[:, columns], axis=0, keepdims=True)
                place = pl.ds(part * count + k, 1)
                total[place, columns] = row + add[place, columns] if add is not None else row

        def work(part, pair, bank, start, follower, pending):
            for tile in range(tiles):
                register = (start + tile) % 2
                if tile + 1 < tiles:
                    push(pair, tile + 1, 1 - register)
                elif follower is not None:
                    push(follower, 0, 1 - register)
                for unit in range(2):
                    k, _ = unit_of(pair, unit)
                    wide = [read(p, part, k, lanes) for p, lanes in pieces_of(tile)]
                    pltpu.matmul_acc_lhs(
                        sums[2 * unit + bank], jnp.concatenate(wide, axis=1), register
                    )
                if tile == 0 and pending is not None:
                    drain(*pending)
            return (start + tiles) % 2

        pending, at = None, 0
        push(0, 0, at)
        for part in range(PARTS):
            ahead(part)
            at = work(part, 0, 0, at, 1, pending)
            odd = at

            @pl.loop(0, (pairs - 2) // 2)
            def _(step):
                now = work(part, 2 * step + 1, 1, odd, 2 * step + 2, (part, 2 * step, 0))
                work(part, 2 * step + 2, 0, now, 2 * step + 3, (part, 2 * step + 1, 1))

            follower = None if part + 1 == PARTS else 0
            at = work(part, pairs - 1, 1, odd, follower, (part, pairs - 2, 0))
            pending = (part, pairs - 1, 1)
        drain(*pending)

    pl.run_scoped(run, *[pltpu.ACC(unit)((modes, width), jnp.float32) for unit in (0, 0, 1, 1)])


def near_kernel(table, mine, mate, tensors, *refs):
    parts, (total, own, far, sems) = refs[:PARTS], refs[PARTS:]
    copies = [
        pltpu.make_async_copy(
            tensors.at[tensor_of(table, 2 + at), pl.ds(0, far.shape[1])], far.at[at], sems.at[at]
        )
        for at in range(2)
    ]
    for copy in copies:
        copy.start()
    own[...] = mine[...].reshape(own.shape[::-1]).astype(jnp.float32).T

    def read(p, part, k, lanes):
        return parts[part][p, k, :, lanes]

    contract(read, parts[0].shape[1], (mine, mate), own, total, None, lambda part: None)
    for copy in copies:
        copy.wait()


def collide_near(table, mine, mate, tensors, parts):
    groups, cells, modes = mine.shape
    out_modes = tensors.shape[1]
    vmem = pl.BlockSpec(memory_space=pltpu.VMEM)
    return pl.pallas_call(
        near_kernel,
        in_specs=[
            pl.BlockSpec(memory_space=pltpu.SMEM),
            vmem,
            vmem,
            pl.BlockSpec(memory_space=pl.ANY),
        ]
        + [vmem] * PARTS,
        out_specs=(vmem, vmem, vmem),
        scratch_shapes=[pltpu.SemaphoreType.DMA((2,))],
        out_shape=(
            pltpu.VMEM((out_modes, groups * cells), jnp.float32),
            pltpu.VMEM((modes, groups * cells), jnp.float32),
            pltpu.VMEM((2, out_modes - out_modes // PARTS) + tensors.shape[2:], tensors.dtype),
        ),
        compiler_params=pltpu.CompilerParams(vmem_limit_bytes=2 * MIB),
        cost_estimate=pl.CostEstimate(
            flops=tensors.size * groups * cells, transcendentals=0, bytes_accessed=tensors.size
        ),
        name="collide_near",
    )(table, close(mine), close(mate), tensors, *[close(part) for part in parts])


def far_kernel(table, one, two, tensors, far, first, own, limiter, out, total, rest, sems):
    count = rest.shape[1]
    copies = [
        pltpu.make_async_copy(
            tensors.at[tensor_of(table, 2 + at), pl.ds(far.shape[1], count)],
            rest.at[at],
            sems.at[at],
        )
        for at in range(2)
    ]
    for copy in copies:
        copy.start()

    def ahead(part):
        if part + 1 == PARTS:
            for copy in copies:
                copy.wait()

    def read(p, part, k, lanes):
        return rest[p, k, :, lanes] if part + 1 == PARTS else far[p, part * count + k, :, lanes]

    contract(read, count, (one, two), own, total, first, ahead)
    groups, cells, _ = one.shape
    here = lax.axis_index("cell")
    whole = total[...].T
    out_modes = whole.shape[1]
    fold = fold_of(cells, out_modes)
    rows = cells // fold
    flag = limiter[:, cells - 1 :].astype(jnp.float32)
    spare = jnp.broadcast_to(flag, (rows, LANES - fold * out_modes))
    for d in range(groups):
        start = d * cells
        parts = [whole[start + f * rows : start + (f + 1) * rows] for f in range(fold)]
        out[here ^ reverse(d, groups)] = jnp.concatenate(parts + [spare], axis=1)


def collide_far(table, one, two, tensors, far, first, own, limiter):
    groups, cells, modes = one.shape
    out_modes = tensors.shape[1]
    rows = cells // fold_of(cells, out_modes)
    vmem = pl.BlockSpec(memory_space=pltpu.VMEM)
    anywhere = pl.BlockSpec(memory_space=pl.ANY)
    return pl.pallas_call(
        far_kernel,
        in_specs=[pl.BlockSpec(memory_space=pltpu.SMEM), vmem, vmem, anywhere] + [vmem] * 4,
        out_specs=vmem,
        scratch_shapes=[
            pltpu.VMEM((out_modes, groups * cells), jnp.float32),
            pltpu.VMEM((2, out_modes // PARTS) + tensors.shape[2:], tensors.dtype),
            pltpu.SemaphoreType.DMA((2,)),
        ],
        out_shape=pltpu.VMEM((groups, rows, LANES), jnp.float32),
        compiler_params=pltpu.CompilerParams(vmem_limit_bytes=11 * MIB),
        cost_estimate=pl.CostEstimate(
            flops=tensors.size * groups * cells, transcendentals=0, bytes_accessed=tensors.size
        ),
        name="collide_far",
    )(table, close(one), close(two), tensors, close(far), close(first), close(own), limiter)


def flux_kernel(mine, limiter, plus, minus, flux):
    groups, cells, modes = mine.shape
    place = lax.axis_index("cell")
    before = slot_of(place, lax.rem(place + groups - 1, groups), groups)
    after = slot_of(place, lax.rem(place + 1, groups), groups)
    wide = jnp.concatenate([mine[d].astype(jnp.float32) for d in (before, 0, after)], axis=0)
    wide = wide[cells - 2 : 2 * cells + 2]
    lower = wide[1:-1] - wide[:-2]
    upper = wide[2:] - wide[1:-1]
    one = minmod_two(lower, upper)
    two = minmod_three(2.0 * lower, 0.5 * (lower + upper), 2.0 * upper)
    flags = column(limiter[...])
    ahead = lax.broadcasted_iota(jnp.int32, (3, 1), 0)

    def chosen(first, second, flag):
        return jnp.where(flag == 1, first, jnp.where(flag == 2, second, 0.0))

    def stack(shift):
        base = wide[1 + shift :]
        faces = base[1 : cells + 1]
        faces = faces + (0.5 - shift) * chosen(
            one[1 + shift : 1 + shift + cells], two[1 + shift : 1 + shift + cells], flags
        )
        edge = base[:1] + (0.5 - shift) * chosen(
            one[shift : shift + 1], two[shift : shift + 1], ahead
        )
        pad = jnp.zeros((flux.shape[0] - cells - 3, modes), jnp.float32)
        return jnp.concatenate([faces, edge, pad], axis=0)

    total = jnp.dot(
        stack(0), plus[0], precision=lax.Precision.HIGHEST, preferred_element_type=jnp.float32
    )
    total = total + jnp.dot(
        stack(1), minus[0], precision=lax.Precision.HIGHEST, preferred_element_type=jnp.float32
    )
    flux[...] = total


def transport(mine, limiter, plus, minus):
    groups, cells, modes = mine.shape
    vmem = pl.BlockSpec(memory_space=pltpu.VMEM)
    return pl.pallas_call(
        flux_kernel,
        in_specs=[vmem, vmem, vmem, vmem],
        out_specs=vmem,
        out_shape=jax.ShapeDtypeStruct((cells + 8, modes), jnp.float32),
        compiler_params=pltpu.CompilerParams(vmem_limit_bytes=4 * MIB),
        name="transport",
    )(close(mine), limiter, plus, minus)


def finish_kernel(out_modes, received, flux, fields, new_field, collision):
    groups, rows, _ = received.shape
    cells = fields.shape[1]
    fold = cells // rows
    parts = []
    for f in range(fold):
        pieces = [received[g][:, f * out_modes : (f + 1) * out_modes] for g in range(groups)]
        parts.append(jnp.concatenate(pieces, axis=1))
    term = jnp.concatenate(parts, axis=0)
    collision[0] = term
    before = lax.rem(lax.axis_index("cell") + groups - 1, groups)
    flag = received[before][:1, fold * out_modes : fold * out_modes + 1]
    behind = flux[cells : cells + 3]
    edge = jnp.where(flag == 1.0, behind[1:2], jnp.where(flag == 2.0, behind[2:3], behind[:1]))
    faces = flux[:cells]
    ahead = jnp.concatenate([edge, faces[:-1]], axis=0)
    new_field[0] = fields[0].astype(jnp.float32) + 0.4 * (ahead - faces) + 0.5 * term


def finish(received, flux, fields, out_modes):
    vmem = pl.BlockSpec(memory_space=pltpu.VMEM)
    shape = jax.ShapeDtypeStruct(fields.shape, jnp.float32)
    return pl.pallas_call(
        functools.partial(finish_kernel, out_modes),
        in_specs=[vmem, vmem, vmem],
        out_specs=(vmem, vmem),
        out_shape=(shape, shape),
        compiler_params=pltpu.CompilerParams(vmem_limit_bytes=4 * MIB),
        name="finish",
    )(received, flux, fields)


def exchanged(x, axis, bit):
    return lax.ppermute(x, axis, [(i, i ^ bit) for i in range(lax.axis_size(axis))])


def local(fields, tensors, pair_table, plus_flux, minus_flux, face_limiter):
    groups = lax.axis_size("cell")
    count = tensors.shape[1] // PARTS
    mine, parts, token = fields, [], None
    bit = groups // 2
    while bit > 0:
        came = exchanged(mine, "cell", bit)
        if len(parts) < PARTS:
            part, token = fetch(pair_table, mine, tensors, len(parts) * count, count)
            parts.append(part)
        mine = join(mine, came, token)
        bit //= 2
    mate = exchanged(mine, "spec", 1)
    far_one = exchanged(mine, "spec", 2)
    far_two = exchanged(mate, "spec", 2)
    first, own, far = collide_near(pair_table, mine, mate, tensors, parts)
    block = collide_far(pair_table, far_one, far_two, tensors, far, first, own, face_limiter)
    received = lax.all_to_all(block, "cell", split_axis=0, concat_axis=0, tiled=False)
    flux = transport(mine, face_limiter, plus_flux, minus_flux)
    return finish(received, flux, fields, tensors.shape[1])


def solution(mesh):
    placed = (
        P("spec", "cell", None),
        P("spec", "cell", None, None),
        P(),
        P("spec", None, None),
        P("spec", None, None),
        P("spec", "cell"),
    )
    return jax.shard_map(
        local,
        mesh=mesh,
        in_specs=placed,
        out_specs=(P("spec", "cell", None), P("spec", "cell", None)),
        check_vma=False,
    )
```

```python
import functools

import jax
import jax.numpy as jnp
from jax import lax
from jax.experimental import pallas as pl
from jax.experimental.pallas import tpu as pltpu
from jax.sharding import PartitionSpec as P

LANES = 128
MIB = 1 << 20
SETS = 3


def minmod_two(first, second):
    least = jnp.minimum(jnp.abs(first), jnp.abs(second))
    return jnp.where(first * second > 0, jnp.where(first > 0, least, -least), 0.0)


def minmod_three(first, second, third):
    same = (first * second > 0) & (second * third > 0)
    least = jnp.minimum(jnp.minimum(jnp.abs(first), jnp.abs(second)), jnp.abs(third))
    return jnp.where(same, jnp.where(first > 0, least, -least), 0.0)


def column(row):
    n = row.shape[1]
    down = lax.broadcasted_iota(jnp.int32, (n, n), 0)
    across = lax.broadcasted_iota(jnp.int32, (n, n), 1)
    return jnp.sum(jnp.where(down == across, row, 0), axis=1, keepdims=True)


def fold_of(cells, out_modes):
    fold = 1
    while cells % (2 * fold) == 0 and 2 * fold * out_modes < LANES:
        fold *= 2
    return fold


def reverse(number, count):
    out, bit = 0, 1
    while bit < count:
        out = out * 2 + number // bit % 2
        bit *= 2
    return out


def slot_of(here, there, groups):
    difference = here ^ there
    out, bit = 0, 0
    while (1 << bit) < groups:
        out = out * 2 + ((difference >> bit) & 1)
        bit += 1
    return out


def close(x):
    return pltpu.with_memory_space_constraint(x, pltpu.VMEM)


def tensor_of(table, partner):
    owner = lax.axis_index("spec")
    return table[owner, owner ^ partner] - owner * table.shape[0]


def fetch_kernel(tensors, *refs, first, count):
    near, token, sem = refs[-3:]
    copy = pltpu.make_async_copy(tensors.at[:, pl.ds(first, count)], near, sem)
    copy.start()
    token[...] = jnp.zeros_like(token)
    copy.wait()


def fetch(after, tensors, first, count):
    shape = (tensors.shape[0], count) + tensors.shape[2:]
    anywhere = pl.BlockSpec(memory_space=pl.ANY)
    vmem = pl.BlockSpec(memory_space=pltpu.VMEM)
    held = [] if after is None else [close(after)]
    return pl.pallas_call(
        functools.partial(fetch_kernel, first=first, count=count),
        in_specs=[anywhere] + [vmem] * len(held),
        out_specs=(vmem, vmem),
        scratch_shapes=[pltpu.SemaphoreType.DMA],
        out_shape=(pltpu.VMEM(shape, tensors.dtype), pltpu.VMEM((8, LANES), jnp.float32)),
        compiler_params=pltpu.CompilerParams(vmem_limit_bytes=MIB),
        cost_estimate=pl.CostEstimate(
            flops=0,
            transcendentals=0,
            bytes_accessed=4 * tensors.shape[0] * count * tensors.shape[2] * tensors.shape[3],
        ),
        name="fetch",
    )(tensors, *held)


def join_kernel(here, came, token, out):
    count = here.shape[0]
    out[:count] = here[...]
    out[count:] = came[...]


def join(here, came, token):
    vmem = pl.BlockSpec(memory_space=pltpu.VMEM)
    return pl.pallas_call(
        join_kernel,
        in_specs=[vmem, vmem, vmem],
        out_specs=vmem,
        out_shape=pltpu.VMEM((2 * here.shape[0],) + here.shape[1:], here.dtype),
        compiler_params=pltpu.CompilerParams(vmem_limit_bytes=MIB),
        name="join",
    )(close(here), close(came), close(token))


def contract(parts, others, own, total, add, ready):
    groups, cells, modes = others[0].shape
    everyone = groups * cells
    width = 2 * LANES
    tiles = len(others) * modes // width
    spans = everyone // width

    def unit_of(pair, unit):
        at = 2 * pair + unit
        if spans == 1:
            return at, 0
        return at // spans, at % spans

    def columns_of(span):
        return slice(0, width) if spans == 1 else pl.ds(pl.multiple_of(span * width, width), width)

    def pieces_of(tile):
        for piece in (2 * tile, 2 * tile + 1):
            yield piece * LANES // modes, slice(piece * LANES % modes, piece * LANES % modes + LANES)

    def push(pair, tile, register):
        for unit in range(2):
            _, span = unit_of(pair, unit)
            of = width // cells
            rows = slice(0, of) if spans == 1 else pl.ds(span * of, of)
            tall = [others[p][rows, :, lanes].reshape(width, LANES) for p, lanes in pieces_of(tile)]
            pltpu.matmul_push_rhs(jnp.concatenate(tall, axis=1), register, unit, transpose=True)

    def run(*sums):
        def drain(part, pair, bank):
            for unit in range(2):
                k, span = unit_of(pair, unit)
                columns = columns_of(span)
                inner = pltpu.matmul_pop(sums[2 * unit + bank])
                row = jnp.sum(inner * own[:, columns], axis=0, keepdims=True)
                place = pl.ds(sum(count for _, count in parts[:part]) + k, 1)
                total[place, columns] = row + add[place, columns] if add is not None else row

        def work(part, pair, bank, start, follower, pending):
            for tile in range(tiles):
                register = (start + tile) % 2
                if tile + 1 < tiles:
                    push(pair, tile + 1, 1 - register)
                elif follower is not None:
                    push(follower, 0, 1 - register)
                for unit in range(2):
                    k, _ = unit_of(pair, unit)
                    wide = [parts[part][0](p, k, lanes) for p, lanes in pieces_of(tile)]
                    pltpu.matmul_acc_lhs(
                        sums[2 * unit + bank], jnp.concatenate(wide, axis=1), register
                    )
                if tile == 0 and pending is not None:
                    drain(*pending)
            return (start + tiles) % 2

        pending, at = None, 0
        push(0, 0, at)
        for part in range(len(parts)):
            last = part + 1 == len(parts)
            pairs = parts[part][1] * spans // 2
            if last:
                ready(0)
            at = work(part, 0, 0, at, 1, pending)
            odd = at

            @pl.loop(0, (pairs - 2) // 2)
            def _(step):
                for number in range(1, SETS if last else 0):

                    @pl.when(step == (number * (pairs // SETS) - 1) // 2)
                    def _():
                        ready(number)

                now = work(part, 2 * step + 1, 1, odd, 2 * step + 2, (part, 2 * step, 0))
                work(part, 2 * step + 2, 0, now, 2 * step + 3, (part, 2 * step + 1, 1))

            follower = None if last else 0
            at = work(part, pairs - 1, 1, odd, follower, (part, pairs - 2, 0))
            pending = (part, pairs - 1, 1)
        drain(*pending)

    pl.run_scoped(run, *[pltpu.ACC(unit)((modes, width), jnp.float32) for unit in (0, 0, 1, 1)])


def stream(table, tensors, held, beside, sems, partners):
    done = sum(ref.shape[1] for ref in held)
    count = beside.shape[1] // SETS
    picks = [tensor_of(table, partner) for partner in partners]

    def copies(number):
        return [
            pltpu.make_async_copy(
                tensors.at[pick, pl.ds(done + number * count, count)],
                beside.at[at, pl.ds(number * count, count)],
                sems.at[at, number],
            )
            for at, pick in enumerate(picks)
        ]

    def start(number):
        for copy in copies(number):
            copy.start()

    def ready(number):
        for copy in copies(number):
            copy.wait()
        if number + 2 < SETS:
            start(number + 2)

    def early(ref):
        return lambda p, k, lanes: ref[picks[p], k, :, lanes]

    def late(p, k, lanes):
        return beside[p, k, :, lanes]

    start(0)
    start(1)
    return [(early(ref), ref.shape[1]) for ref in held] + [(late, beside.shape[1])], ready


def near_kernel(table, mine, mate, tensors, *refs):
    held, (total, own, beside, sems) = refs[:SETS], refs[SETS:]
    parts, ready = stream(table, tensors, held, beside, sems, (0, 1))
    own[...] = mine[...].reshape(own.shape[::-1]).astype(jnp.float32).T
    contract(parts, (mine, mate), own, total, None, ready)


def streamed(tensors, held):
    left = tensors.shape[1] - sum(part.shape[1] for part in held)
    return [
        pltpu.VMEM((2, left) + tensors.shape[2:], tensors.dtype),
        pltpu.SemaphoreType.DMA((2, SETS)),
    ]


def collide_near(table, mine, mate, tensors, held):
    groups, cells, modes = mine.shape
    out_modes = tensors.shape[1]
    vmem = pl.BlockSpec(memory_space=pltpu.VMEM)
    anywhere = pl.BlockSpec(memory_space=pl.ANY)
    return pl.pallas_call(
        near_kernel,
        in_specs=[pl.BlockSpec(memory_space=pltpu.SMEM), vmem, vmem, anywhere] + [vmem] * SETS,
        out_specs=(vmem, vmem),
        scratch_shapes=streamed(tensors, held),
        out_shape=(
            pltpu.VMEM((out_modes, groups * cells), jnp.float32),
            pltpu.VMEM((modes, groups * cells), jnp.float32),
        ),
        compiler_params=pltpu.CompilerParams(vmem_limit_bytes=16 * MIB),
        cost_estimate=pl.CostEstimate(
            flops=tensors.size * groups * cells, transcendentals=0, bytes_accessed=tensors.size
        ),
        name="collide_near",
    )(table, close(mine), close(mate), tensors, *[close(part) for part in held])


def far_kernel(table, one, two, tensors, *refs):
    held, (first, own, limiter, out, total, beside, sems) = refs[:SETS], refs[SETS:]
    parts, ready = stream(table, tensors, held, beside, sems, (2, 3))
    contract(parts, (one, two), own, total, first, ready)
    groups, cells, _ = one.shape
    here = lax.axis_index("cell")
    whole = total[...].T
    out_modes = whole.shape[1]
    fold = fold_of(cells, out_modes)
    rows = cells // fold
    flag = limiter[:, cells - 1 :].astype(jnp.float32)
    spare = jnp.broadcast_to(flag, (rows, LANES - fold * out_modes))
    for d in range(groups):
        start = d * cells
        parts = [whole[start + f * rows : start + (f + 1) * rows] for f in range(fold)]
        out[here ^ reverse(d, groups)] = jnp.concatenate(parts + [spare], axis=1)


def collide_far(table, one, two, tensors, held, first, own, limiter):
    groups, cells, modes = one.shape
    out_modes = tensors.shape[1]
    rows = cells // fold_of(cells, out_modes)
    vmem = pl.BlockSpec(memory_space=pltpu.VMEM)
    anywhere = pl.BlockSpec(memory_space=pl.ANY)
    return pl.pallas_call(
        far_kernel,
        in_specs=[pl.BlockSpec(memory_space=pltpu.SMEM), vmem, vmem, anywhere] + [vmem] * (SETS + 3),
        out_specs=vmem,
        scratch_shapes=[
            pltpu.VMEM((out_modes, groups * cells), jnp.float32),
            *streamed(tensors, held),
        ],
        out_shape=pltpu.VMEM((groups, rows, LANES), jnp.float32),
        compiler_params=pltpu.CompilerParams(vmem_limit_bytes=16 * MIB),
        cost_estimate=pl.CostEstimate(
            flops=tensors.size * groups * cells, transcendentals=0, bytes_accessed=tensors.size
        ),
        name="collide_far",
    )(
        table,
        close(one),
        close(two),
        tensors,
        *[close(part) for part in held],
        close(first),
        close(own),
        limiter,
    )


def flux_kernel(mine, limiter, plus, minus, flux):
    groups, cells, modes = mine.shape
    place = lax.axis_index("cell")
    before = slot_of(place, lax.rem(place + groups - 1, groups), groups)
    after = slot_of(place, lax.rem(place + 1, groups), groups)
    wide = jnp.concatenate([mine[d].astype(jnp.float32) for d in (before, 0, after)], axis=0)
    wide = wide[cells - 2 : 2 * cells + 2]
    lower = wide[1:-1] - wide[:-2]
    upper = wide[2:] - wide[1:-1]
    one = minmod_two(lower, upper)
    two = minmod_three(2.0 * lower, 0.5 * (lower + upper), 2.0 * upper)
    flags = column(limiter[...])
    ahead = lax.broadcasted_iota(jnp.int32, (3, 1), 0)

    def chosen(first, second, flag):
        return jnp.where(flag == 1, first, jnp.where(flag == 2, second, 0.0))

    def stack(shift):
        base = wide[1 + shift :]
        faces = base[1 : cells + 1]
        faces = faces + (0.5 - shift) * chosen(
            one[1 + shift : 1 + shift + cells], two[1 + shift : 1 + shift + cells], flags
        )
        edge = base[:1] + (0.5 - shift) * chosen(
            one[shift : shift + 1], two[shift : shift + 1], ahead
        )
        pad = jnp.zeros((flux.shape[0] - cells - 3, modes), jnp.float32)
        return jnp.concatenate([faces, edge, pad], axis=0)

    total = jnp.dot(
        stack(0), plus[0], precision=lax.Precision.HIGHEST, preferred_element_type=jnp.float32
    )
    total = total + jnp.dot(
        stack(1), minus[0], precision=lax.Precision.HIGHEST, preferred_element_type=jnp.float32
    )
    flux[...] = total


def transport(mine, limiter, plus, minus):
    groups, cells, modes = mine.shape
    vmem = pl.BlockSpec(memory_space=pltpu.VMEM)
    return pl.pallas_call(
        flux_kernel,
        in_specs=[vmem, vmem, vmem, vmem],
        out_specs=vmem,
        out_shape=jax.ShapeDtypeStruct((cells + 8, modes), jnp.float32),
        compiler_params=pltpu.CompilerParams(vmem_limit_bytes=4 * MIB),
        name="transport",
    )(close(mine), limiter, plus, minus)


def finish_kernel(out_modes, received, flux, fields, new_field, collision):
    groups, rows, _ = received.shape
    cells = fields.shape[1]
    fold = cells // rows
    parts = []
    for f in range(fold):
        pieces = [received[g][:, f * out_modes : (f + 1) * out_modes] for g in range(groups)]
        parts.append(jnp.concatenate(pieces, axis=1))
    term = jnp.concatenate(parts, axis=0)
    collision[0] = term
    before = lax.rem(lax.axis_index("cell") + groups - 1, groups)
    flag = received[before][:1, fold * out_modes : fold * out_modes + 1]
    behind = flux[cells : cells + 3]
    edge = jnp.where(flag == 1.0, behind[1:2], jnp.where(flag == 2.0, behind[2:3], behind[:1]))
    faces = flux[:cells]
    ahead = jnp.concatenate([edge, faces[:-1]], axis=0)
    new_field[0] = fields[0].astype(jnp.float32) + 0.4 * (ahead - faces) + 0.5 * term


def finish(received, flux, fields, out_modes):
    vmem = pl.BlockSpec(memory_space=pltpu.VMEM)
    shape = jax.ShapeDtypeStruct(fields.shape, jnp.float32)
    return pl.pallas_call(
        functools.partial(finish_kernel, out_modes),
        in_specs=[vmem, vmem, vmem],
        out_specs=(vmem, vmem),
        out_shape=(shape, shape),
        compiler_params=pltpu.CompilerParams(vmem_limit_bytes=4 * MIB),
        name="finish",
    )(received, flux, fields)


def exchanged(x, axis, bit):
    return lax.ppermute(x, axis, [(i, i ^ bit) for i in range(lax.axis_size(axis))])


def local(fields, tensors, pair_table, plus_flux, minus_flux, face_limiter):
    groups = lax.axis_size("cell")
    count = tensors.shape[1] // (2 * SETS)
    mine, held, token = fields, [], None
    bit = groups // 2
    while bit > 0:
        came = exchanged(mine, "cell", bit)
        if len(held) < SETS:
            part, token = fetch(mine if held else None, tensors, len(held) * count, count)
            held.append(part)
        mine = join(mine, came, token)
        bit //= 2
    while len(held) < SETS:
        held.append(fetch(mine, tensors, len(held) * count, count)[0])
    mate = exchanged(mine, "spec", 1)
    far_one = exchanged(mine, "spec", 2)
    far_two = exchanged(mate, "spec", 2)
    first, own = collide_near(pair_table, mine, mate, tensors, held)
    block = collide_far(pair_table, far_one, far_two, tensors, held, first, own, face_limiter)
    received = lax.all_to_all(block, "cell", split_axis=0, concat_axis=0, tiled=False)
    flux = transport(mine, face_limiter, plus_flux, minus_flux)
    return finish(received, flux, fields, tensors.shape[1])


def solution(mesh):
    placed = (
        P("spec", "cell", None),
        P("spec", "cell", None, None),
        P(),
        P("spec", None, None),
        P("spec", None, None),
        P("spec", "cell"),
    )
    return jax.shard_map(
        local,
        mesh=mesh,
        in_specs=placed,
        out_specs=(P("spec", "cell", None), P("spec", "cell", None)),
        check_vma=False,
    )
```

```python
import functools

import jax
import jax.numpy as jnp
from jax import lax
from jax.experimental import pallas as pl
from jax.experimental.pallas import tpu as pltpu
from jax.sharding import PartitionSpec as P

LANES = 128
MIB = 1 << 20
SIXTHS = 6


def minmod_two(first, second):
    least = jnp.minimum(jnp.abs(first), jnp.abs(second))
    return jnp.where(first * second > 0, jnp.where(first > 0, least, -least), 0.0)


def minmod_three(first, second, third):
    same = (first * second > 0) & (second * third > 0)
    least = jnp.minimum(jnp.minimum(jnp.abs(first), jnp.abs(second)), jnp.abs(third))
    return jnp.where(same, jnp.where(first > 0, least, -least), 0.0)


def column(row):
    n = row.shape[1]
    down = lax.broadcasted_iota(jnp.int32, (n, n), 0)
    across = lax.broadcasted_iota(jnp.int32, (n, n), 1)
    return jnp.sum(jnp.where(down == across, row, 0), axis=1, keepdims=True)


def fold_of(cells, out_modes):
    fold = 1
    while cells % (2 * fold) == 0 and 2 * fold * out_modes < LANES:
        fold *= 2
    return fold


def reverse(number, count):
    out, bit = 0, 1
    while bit < count:
        out = out * 2 + number // bit % 2
        bit *= 2
    return out


def slot_of(here, there, groups):
    difference = here ^ there
    out, bit = 0, 0
    while (1 << bit) < groups:
        out = out * 2 + ((difference >> bit) & 1)
        bit += 1
    return out


def close(x):
    return pltpu.with_memory_space_constraint(x, pltpu.VMEM)


def tensor_of(table, partner):
    owner = lax.axis_index("spec")
    return table[owner, owner ^ partner] - owner * table.shape[0]


def copies_of(table, tensors, partners, first, near, sems):
    modes = pl.ds(first, near.shape[1])
    return [
        pltpu.make_async_copy(
            tensors.at[tensor_of(table, partner), modes], near.at[at], sems.at[at]
        )
        for at, partner in enumerate(partners)
    ]


def start_all(copies):
    for copy in copies:
        copy.start()


def wait_all(copies):
    for copy in copies:
        copy.wait()


def fetch_all_kernel(tensors, near, token, sem):
    copy = pltpu.make_async_copy(tensors.at[:, pl.ds(0, near.shape[1])], near, sem)
    copy.start()
    token[...] = jnp.zeros_like(token)
    copy.wait()


def fetch_near_kernel(table, after, tensors, near, token, sems, *, first):
    copies = copies_of(table, tensors, (0, 1), first, near, sems)
    start_all(copies)
    token[...] = jnp.zeros_like(token)
    wait_all(copies)


def fetch(kernel, operands, specs, tensors, species, count, sems):
    shape = (species, count) + tensors.shape[2:]
    vmem = pl.BlockSpec(memory_space=pltpu.VMEM)
    return pl.pallas_call(
        kernel,
        in_specs=specs + [pl.BlockSpec(memory_space=pl.ANY)],
        out_specs=(vmem, vmem),
        scratch_shapes=[sems],
        out_shape=(pltpu.VMEM(shape, tensors.dtype), pltpu.VMEM((8, LANES), jnp.float32)),
        compiler_params=pltpu.CompilerParams(vmem_limit_bytes=MIB),
        cost_estimate=pl.CostEstimate(
            flops=0,
            transcendentals=0,
            bytes_accessed=4 * species * count * tensors.shape[2] * tensors.shape[3],
        ),
        name="fetch",
    )(*operands, tensors)


def fetch_all(tensors, count):
    return fetch(
        fetch_all_kernel, [], [], tensors, tensors.shape[0], count, pltpu.SemaphoreType.DMA
    )


def fetch_near(table, after, tensors, first, count):
    specs = [pl.BlockSpec(memory_space=pltpu.SMEM), pl.BlockSpec(memory_space=pltpu.VMEM)]
    return fetch(
        functools.partial(fetch_near_kernel, first=first),
        [table, close(after)],
        specs,
        tensors,
        2,
        count,
        pltpu.SemaphoreType.DMA((2,)),
    )


def join_kernel(here, came, token, out):
    count = here.shape[0]
    out[:count] = here[...]
    out[count:] = came[...]


def join(here, came, token):
    vmem = pl.BlockSpec(memory_space=pltpu.VMEM)
    return pl.pallas_call(
        join_kernel,
        in_specs=[vmem, vmem, vmem],
        out_specs=vmem,
        out_shape=pltpu.VMEM((2 * here.shape[0],) + here.shape[1:], here.dtype),
        compiler_params=pltpu.CompilerParams(vmem_limit_bytes=MIB),
        name="join",
    )(close(here), close(came), close(token))


def contract(parts, others, own, total, add):
    groups, cells, modes = others[0].shape
    everyone = groups * cells
    width = 2 * LANES
    tiles = len(others) * modes // width
    spans = everyone // width

    def unit_of(pair, unit):
        at = 2 * pair + unit
        if spans == 1:
            return at, 0
        return at // spans, at % spans

    def columns_of(span):
        return slice(0, width) if spans == 1 else pl.ds(pl.multiple_of(span * width, width), width)

    def pieces_of(tile):
        for piece in (2 * tile, 2 * tile + 1):
            yield piece * LANES // modes, slice(piece * LANES % modes, piece * LANES % modes + LANES)

    def push(pair, tile, register):
        for unit in range(2):
            _, span = unit_of(pair, unit)
            of = width // cells
            rows = slice(0, of) if spans == 1 else pl.ds(span * of, of)
            tall = [others[p][rows, :, lanes].reshape(width, LANES) for p, lanes in pieces_of(tile)]
            pltpu.matmul_push_rhs(jnp.concatenate(tall, axis=1), register, unit, transpose=True)

    def run(*sums):
        def drain(part, pair, bank):
            for unit in range(2):
                k, span = unit_of(pair, unit)
                columns = columns_of(span)
                inner = pltpu.matmul_pop(sums[2 * unit + bank])
                row = jnp.sum(inner * own[:, columns], axis=0, keepdims=True)
                place = pl.ds(sum(count for _, count, _ in parts[:part]) + k, 1)
                total[place, columns] = row + add[place, columns] if add is not None else row

        def work(part, pair, bank, start, follower, pending):
            for tile in range(tiles):
                register = (start + tile) % 2
                if tile + 1 < tiles:
                    push(pair, tile + 1, 1 - register)
                elif follower is not None:
                    push(follower, 0, 1 - register)
                for unit in range(2):
                    k, _ = unit_of(pair, unit)
                    wide = [parts[part][0](p, k, lanes) for p, lanes in pieces_of(tile)]
                    pltpu.matmul_acc_lhs(
                        sums[2 * unit + bank], jnp.concatenate(wide, axis=1), register
                    )
                if tile == 0 and pending is not None:
                    drain(*pending)
            return (start + tiles) % 2

        pending, at = None, 0
        push(0, 0, at)
        for part in range(len(parts)):
            last = part + 1 == len(parts)
            pairs = parts[part][1] * spans // 2
            parts[part][2]()
            at = work(part, 0, 0, at, 1, pending)
            odd = at

            @pl.loop(0, (pairs - 2) // 2)
            def _(step):
                now = work(part, 2 * step + 1, 1, odd, 2 * step + 2, (part, 2 * step, 0))
                work(part, 2 * step + 2, 0, now, 2 * step + 3, (part, 2 * step + 1, 1))

            follower = None if last else 0
            at = work(part, pairs - 1, 1, odd, follower, (part, pairs - 2, 0))
            pending = (part, pairs - 1, 1)
        drain(*pending)

    pl.run_scoped(run, *[pltpu.ACC(unit)((modes, width), jnp.float32) for unit in (0, 0, 1, 1)])


def part_of(ref, picks=None, shift=0, count=None, before=lambda: None):
    def read(p, k, lanes):
        return ref[p if picks is None else picks[p], shift + k, :, lanes]

    return read, ref.shape[1] if count is None else count, before


def near_kernel(
    table, mine, mate, tensors, shared, two, three, total, own, far, beside, far_sems, sems
):
    first = shared.shape[1]
    last = copies_of(table, tensors, (0, 1), tensors.shape[1] - first, beside, sems)
    later = copies_of(table, tensors, (2, 3), first, far, far_sems)
    start_all(last + later)
    own[...] = mine[...].reshape(own.shape[::-1]).astype(jnp.float32).T
    picks = [tensor_of(table, partner) for partner in (0, 1)]
    parts = [part_of(shared, picks), part_of(two), part_of(three)]
    parts.append(part_of(beside, before=lambda: wait_all(last)))
    contract(parts, (mine, mate), own, total, None)
    wait_all(later)


def collide_near(table, mine, mate, tensors, shared, two, three):
    groups, cells, modes = mine.shape
    out_modes = tensors.shape[1]
    ahead = out_modes // 2
    vmem = pl.BlockSpec(memory_space=pltpu.VMEM)
    anywhere = pl.BlockSpec(memory_space=pl.ANY)
    return pl.pallas_call(
        near_kernel,
        in_specs=[pl.BlockSpec(memory_space=pltpu.SMEM), vmem, vmem, anywhere] + [vmem] * 3,
        out_specs=(vmem, vmem, vmem),
        scratch_shapes=[
            pltpu.VMEM((2, shared.shape[1]) + tensors.shape[2:], tensors.dtype),
            pltpu.SemaphoreType.DMA((2,)),
            pltpu.SemaphoreType.DMA((2,)),
        ],
        out_shape=(
            pltpu.VMEM((out_modes, groups * cells), jnp.float32),
            pltpu.VMEM((modes, groups * cells), jnp.float32),
            pltpu.VMEM((2, ahead) + tensors.shape[2:], tensors.dtype),
        ),
        compiler_params=pltpu.CompilerParams(vmem_limit_bytes=7 * MIB),
        cost_estimate=pl.CostEstimate(
            flops=tensors.size * groups * cells, transcendentals=0, bytes_accessed=tensors.size
        ),
        name="collide_near",
    )(table, close(mine), close(mate), tensors, close(shared), close(two), close(three))


def far_kernel(
    table, one, two, tensors, shared, far, first, own, limiter, out, total, beside, sems
):
    last = copies_of(table, tensors, (2, 3), tensors.shape[1] - beside.shape[1], beside, sems)
    start_all(last)
    picks = [tensor_of(table, partner) for partner in (2, 3)]
    parts = [part_of(shared, picks), part_of(far)]
    parts.append(part_of(beside, before=lambda: wait_all(last)))
    contract(parts, (one, two), own, total, first)
    groups, cells, _ = one.shape
    here = lax.axis_index("cell")
    whole = total[...].T
    out_modes = whole.shape[1]
    fold = fold_of(cells, out_modes)
    rows = cells // fold
    flag = limiter[:, cells - 1 :].astype(jnp.float32)
    spare = jnp.broadcast_to(flag, (rows, LANES - fold * out_modes))
    for d in range(groups):
        start = d * cells
        parts = [whole[start + f * rows : start + (f + 1) * rows] for f in range(fold)]
        out[here ^ reverse(d, groups)] = jnp.concatenate(parts + [spare], axis=1)


def collide_far(table, one, two, tensors, shared, far, first, own, limiter):
    groups, cells, modes = one.shape
    out_modes = tensors.shape[1]
    rows = cells // fold_of(cells, out_modes)
    left = out_modes - shared.shape[1] - far.shape[1]
    vmem = pl.BlockSpec(memory_space=pltpu.VMEM)
    anywhere = pl.BlockSpec(memory_space=pl.ANY)
    return pl.pallas_call(
        far_kernel,
        in_specs=[pl.BlockSpec(memory_space=pltpu.SMEM), vmem, vmem, anywhere] + [vmem] * 5,
        out_specs=vmem,
        scratch_shapes=[
            pltpu.VMEM((out_modes, groups * cells), jnp.float32),
            pltpu.VMEM((2, left) + tensors.shape[2:], tensors.dtype),
            pltpu.SemaphoreType.DMA((2,)),
        ],
        out_shape=pltpu.VMEM((groups, rows, LANES), jnp.float32),
        compiler_params=pltpu.CompilerParams(vmem_limit_bytes=11 * MIB),
        cost_estimate=pl.CostEstimate(
            flops=tensors.size * groups * cells, transcendentals=0, bytes_accessed=tensors.size
        ),
        name="collide_far",
    )(
        table,
        close(one),
        close(two),
        tensors,
        close(shared),
        close(far),
        close(first),
        close(own),
        limiter,
    )


def flux_kernel(mine, limiter, plus, minus, flux):
    groups, cells, modes = mine.shape
    place = lax.axis_index("cell")
    before = slot_of(place, lax.rem(place + groups - 1, groups), groups)
    after = slot_of(place, lax.rem(place + 1, groups), groups)
    wide = jnp.concatenate([mine[d].astype(jnp.float32) for d in (before, 0, after)], axis=0)
    wide = wide[cells - 2 : 2 * cells + 2]
    lower = wide[1:-1] - wide[:-2]
    upper = wide[2:] - wide[1:-1]
    one = minmod_two(lower, upper)
    two = minmod_three(2.0 * lower, 0.5 * (lower + upper), 2.0 * upper)
    flags = column(limiter[...])
    ahead = lax.broadcasted_iota(jnp.int32, (3, 1), 0)

    def chosen(first, second, flag):
        return jnp.where(flag == 1, first, jnp.where(flag == 2, second, 0.0))

    def stack(shift):
        base = wide[1 + shift :]
        faces = base[1 : cells + 1]
        faces = faces + (0.5 - shift) * chosen(
            one[1 + shift : 1 + shift + cells], two[1 + shift : 1 + shift + cells], flags
        )
        edge = base[:1] + (0.5 - shift) * chosen(
            one[shift : shift + 1], two[shift : shift + 1], ahead
        )
        pad = jnp.zeros((flux.shape[0] - cells - 3, modes), jnp.float32)
        return jnp.concatenate([faces, edge, pad], axis=0)

    total = jnp.dot(
        stack(0), plus[0], precision=lax.Precision.HIGHEST, preferred_element_type=jnp.float32
    )
    total = total + jnp.dot(
        stack(1), minus[0], precision=lax.Precision.HIGHEST, preferred_element_type=jnp.float32
    )
    flux[...] = total


def transport(mine, limiter, plus, minus):
    groups, cells, modes = mine.shape
    vmem = pl.BlockSpec(memory_space=pltpu.VMEM)
    return pl.pallas_call(
        flux_kernel,
        in_specs=[vmem, vmem, vmem, vmem],
        out_specs=vmem,
        out_shape=jax.ShapeDtypeStruct((cells + 8, modes), jnp.float32),
        compiler_params=pltpu.CompilerParams(vmem_limit_bytes=4 * MIB),
        name="transport",
    )(close(mine), limiter, plus, minus)


def finish_kernel(out_modes, received, flux, fields, new_field, collision):
    groups, rows, _ = received.shape
    cells = fields.shape[1]
    fold = cells // rows
    parts = []
    for f in range(fold):
        pieces = [received[g][:, f * out_modes : (f + 1) * out_modes] for g in range(groups)]
        parts.append(jnp.concatenate(pieces, axis=1))
    term = jnp.concatenate(parts, axis=0)
    collision[0] = term
    before = lax.rem(lax.axis_index("cell") + groups - 1, groups)
    flag = received[before][:1, fold * out_modes : fold * out_modes + 1]
    behind = flux[cells : cells + 3]
    edge = jnp.where(flag == 1.0, behind[1:2], jnp.where(flag == 2.0, behind[2:3], behind[:1]))
    faces = flux[:cells]
    ahead = jnp.concatenate([edge, faces[:-1]], axis=0)
    new_field[0] = fields[0].astype(jnp.float32) + 0.4 * (ahead - faces) + 0.5 * term


def finish(received, flux, fields, out_modes):
    vmem = pl.BlockSpec(memory_space=pltpu.VMEM)
    shape = jax.ShapeDtypeStruct(fields.shape, jnp.float32)
    return pl.pallas_call(
        functools.partial(finish_kernel, out_modes),
        in_specs=[vmem, vmem, vmem],
        out_specs=(vmem, vmem),
        out_shape=(shape, shape),
        compiler_params=pltpu.CompilerParams(vmem_limit_bytes=4 * MIB),
        name="finish",
    )(received, flux, fields)


def exchanged(x, axis, bit):
    return lax.ppermute(x, axis, [(i, i ^ bit) for i in range(lax.axis_size(axis))])


def local(fields, tensors, pair_table, plus_flux, minus_flux, face_limiter):
    groups = lax.axis_size("cell")
    count = tensors.shape[1] // SIXTHS
    mine, held, token = fields, [], None

    def more():
        if not held:
            return fetch_all(tensors, count)
        return fetch_near(pair_table, mine, tensors, (2 * len(held) - 1) * count, 2 * count)

    bit = groups // 2
    while bit > 0:
        came = exchanged(mine, "cell", bit)
        if len(held) < 3:
            part, token = more()
            held.append(part)
        mine = join(mine, came, token)
        bit //= 2
    while len(held) < 3:
        held.append(more()[0])
    mate = exchanged(mine, "spec", 1)
    far_one = exchanged(mine, "spec", 2)
    far_two = exchanged(mate, "spec", 2)
    first, own, far = collide_near(pair_table, mine, mate, tensors, *held)
    block = collide_far(
        pair_table, far_one, far_two, tensors, held[0], far, first, own, face_limiter
    )
    received = lax.all_to_all(block, "cell", split_axis=0, concat_axis=0, tiled=False)
    flux = transport(mine, face_limiter, plus_flux, minus_flux)
    return finish(received, flux, fields, tensors.shape[1])


def solution(mesh):
    placed = (
        P("spec", "cell", None),
        P("spec", "cell", None, None),
        P(),
        P("spec", None, None),
        P("spec", None, None),
        P("spec", "cell"),
    )
    return jax.shard_map(
        local,
        mesh=mesh,
        in_specs=placed,
        out_specs=(P("spec", "cell", None), P("spec", "cell", None)),
        check_vma=False,
    )
```

```python
import functools

import jax
import jax.numpy as jnp
from jax import lax
from jax.experimental import pallas as pl
from jax.experimental.pallas import tpu as pltpu
from jax.sharding import PartitionSpec as P

LANES = 128
MIB = 1 << 20
SIXTHS = 6


def minmod_two(first, second):
    least = jnp.minimum(jnp.abs(first), jnp.abs(second))
    return jnp.where(first * second > 0, jnp.where(first > 0, least, -least), 0.0)


def minmod_three(first, second, third):
    same = (first * second > 0) & (second * third > 0)
    least = jnp.minimum(jnp.minimum(jnp.abs(first), jnp.abs(second)), jnp.abs(third))
    return jnp.where(same, jnp.where(first > 0, least, -least), 0.0)


def column(row):
    n = row.shape[1]
    down = lax.broadcasted_iota(jnp.int32, (n, n), 0)
    across = lax.broadcasted_iota(jnp.int32, (n, n), 1)
    return jnp.sum(jnp.where(down == across, row, 0), axis=1, keepdims=True)


def fold_of(cells, out_modes):
    fold = 1
    while cells % (2 * fold) == 0 and 2 * fold * out_modes < LANES:
        fold *= 2
    return fold


def reverse(number, count):
    out, bit = 0, 1
    while bit < count:
        out = out * 2 + number // bit % 2
        bit *= 2
    return out


def slot_of(here, there, groups):
    difference = here ^ there
    out, bit = 0, 0
    while (1 << bit) < groups:
        out = out * 2 + ((difference >> bit) & 1)
        bit += 1
    return out


def close(x):
    return pltpu.with_memory_space_constraint(x, pltpu.VMEM)


def tensor_of(table, partner):
    owner = lax.axis_index("spec")
    return table[owner, owner ^ partner] - owner * table.shape[0]


def copies_of(table, tensors, partners, first, near, sems):
    modes = pl.ds(first, near.shape[1])
    return [
        pltpu.make_async_copy(
            tensors.at[tensor_of(table, partner), modes], near.at[at], sems.at[at]
        )
        for at, partner in enumerate(partners)
    ]


def start_all(copies):
    for copy in copies:
        copy.start()


def wait_all(copies):
    for copy in copies:
        copy.wait()


def fetch_all_kernel(*refs, first):
    tensors, near, token, sem = refs[-4:]
    copy = pltpu.make_async_copy(tensors.at[:, pl.ds(first, near.shape[1])], near, sem)
    copy.start()
    token[...] = jnp.zeros_like(token)
    copy.wait()


def fetch_near_kernel(table, after, tensors, near, token, sems, *, first):
    copies = copies_of(table, tensors, (0, 1), first, near, sems)
    start_all(copies)
    token[...] = jnp.zeros_like(token)
    wait_all(copies)


def fetch(kernel, operands, specs, tensors, species, count, sems):
    shape = (species, count) + tensors.shape[2:]
    vmem = pl.BlockSpec(memory_space=pltpu.VMEM)
    return pl.pallas_call(
        kernel,
        in_specs=specs + [pl.BlockSpec(memory_space=pl.ANY)],
        out_specs=(vmem, vmem),
        scratch_shapes=[sems],
        out_shape=(pltpu.VMEM(shape, tensors.dtype), pltpu.VMEM((8, LANES), jnp.float32)),
        compiler_params=pltpu.CompilerParams(vmem_limit_bytes=MIB),
        cost_estimate=pl.CostEstimate(
            flops=0,
            transcendentals=0,
            bytes_accessed=4 * species * count * tensors.shape[2] * tensors.shape[3],
        ),
        name="fetch",
    )(*operands, tensors)


def fetch_all(after, tensors, first, count):
    operands = [] if after is None else [close(after)]
    return fetch(
        functools.partial(fetch_all_kernel, first=first),
        operands,
        [pl.BlockSpec(memory_space=pltpu.VMEM)] * len(operands),
        tensors,
        tensors.shape[0],
        count,
        pltpu.SemaphoreType.DMA,
    )


def fetch_near(table, after, tensors, first, count):
    specs = [pl.BlockSpec(memory_space=pltpu.SMEM), pl.BlockSpec(memory_space=pltpu.VMEM)]
    return fetch(
        functools.partial(fetch_near_kernel, first=first),
        [table, close(after)],
        specs,
        tensors,
        2,
        count,
        pltpu.SemaphoreType.DMA((2,)),
    )


def join_kernel(here, came, token, out):
    count = here.shape[0]
    out[:count] = here[...]
    out[count:] = came[...]


def join(here, came, token):
    vmem = pl.BlockSpec(memory_space=pltpu.VMEM)
    return pl.pallas_call(
        join_kernel,
        in_specs=[vmem, vmem, vmem],
        out_specs=vmem,
        out_shape=pltpu.VMEM((2 * here.shape[0],) + here.shape[1:], here.dtype),
        compiler_params=pltpu.CompilerParams(vmem_limit_bytes=MIB),
        name="join",
    )(close(here), close(came), close(token))


def contract(parts, others, own, total, add):
    groups, cells, modes = others[0].shape
    everyone = groups * cells
    width = 2 * LANES
    tiles = len(others) * modes // width
    spans = everyone // width

    def unit_of(group, bank, unit):
        if spans == 1:
            return 4 * group + 2 * bank + unit, 0
        at = 2 * group + unit
        return at // spans * 2 + bank, at % spans

    def columns_of(span):
        return slice(0, width) if spans == 1 else pl.ds(pl.multiple_of(span * width, width), width)

    def pieces_of(tile):
        for piece in (2 * tile, 2 * tile + 1):
            yield piece * LANES // modes, slice(piece * LANES % modes, piece * LANES % modes + LANES)

    def push(group, tile, register):
        for unit in range(2):
            _, span = unit_of(group, 0, unit)
            of = width // cells
            rows = slice(0, of) if spans == 1 else pl.ds(span * of, of)
            tall = [others[p][rows, :, lanes].reshape(width, LANES) for p, lanes in pieces_of(tile)]
            pltpu.matmul_push_rhs(jnp.concatenate(tall, axis=1), register, unit, transpose=True)

    def run(*sums):
        def drain(part, group, bank):
            for unit in range(2):
                k, span = unit_of(group, bank, unit)
                columns = columns_of(span)
                inner = pltpu.matmul_pop(sums[2 * unit + bank])
                row = jnp.sum(inner * own[:, columns], axis=0, keepdims=True)
                place = pl.ds(sum(count for _, count, _ in parts[:part]) + k, 1)
                total[place, columns] = row + add[place, columns] if add is not None else row

        def work(part, group, start, follower, pending):
            for tile in range(tiles):
                register = (start + tile) % 2
                if tile + 1 < tiles:
                    push(group, tile + 1, 1 - register)
                elif follower is not None:
                    push(follower, 0, 1 - register)
                for bank in range(2):
                    for unit in range(2):
                        k, _ = unit_of(group, bank, unit)
                        wide = [parts[part][0](p, k, lanes) for p, lanes in pieces_of(tile)]
                        pltpu.matmul_acc_lhs(
                            sums[2 * unit + bank],
                            jnp.concatenate(wide, axis=1),
                            register if bank == 0 else None,
                        )
                    if bank == 0 and tile == 0 and pending is not None:
                        drain(*pending, 1)
            drain(part, group, 0)
            return (start + tiles) % 2

        pending, at = None, 0
        push(0, 0, at)
        for part in range(len(parts)):
            last = part + 1 == len(parts)
            groups_here = parts[part][1] * spans // 4
            parts[part][2]()
            at = work(part, 0, at, 1, pending)
            odd = at

            if groups_here > 2:

                @pl.loop(0, (groups_here - 2) // 2)
                def _(step):
                    now = work(part, 2 * step + 1, odd, 2 * step + 2, (part, 2 * step))
                    work(part, 2 * step + 2, now, 2 * step + 3, (part, 2 * step + 1))

            follower = None if last else 0
            at = work(part, groups_here - 1, odd, follower, (part, groups_here - 2))
            pending = (part, groups_here - 1)
        drain(*pending, 1)

    pl.run_scoped(run, *[pltpu.ACC(unit)((modes, width), jnp.float32) for unit in (0, 0, 1, 1)])


def part_of(ref, picks=None, shift=0, count=None, before=lambda: None):
    def read(p, k, lanes):
        return ref[p if picks is None else picks[p], shift + k, :, lanes]

    return read, ref.shape[1] if count is None else count, before


def near_kernel(
    table, mine, mate, tensors, one, two, three, total, own, far, beside, far_sems, sems
):
    ahead = one.shape[1] + two.shape[1]
    last = copies_of(table, tensors, (0, 1), ahead + three.shape[1], beside, sems)
    later = copies_of(table, tensors, (2, 3), ahead, far, far_sems)
    start_all(last)
    own[...] = mine[...].reshape(own.shape[::-1]).astype(jnp.float32).T
    picks = [tensor_of(table, partner) for partner in (0, 1)]
    parts = [
        part_of(one, picks),
        part_of(two, picks),
        part_of(three, before=lambda: start_all(later)),
        part_of(beside, before=lambda: wait_all(last)),
    ]
    contract(parts, (mine, mate), own, total, None)
    wait_all(later)


def collide_near(table, mine, mate, tensors, one, two, three):
    groups, cells, modes = mine.shape
    out_modes = tensors.shape[1]
    count = three.shape[1]
    vmem = pl.BlockSpec(memory_space=pltpu.VMEM)
    anywhere = pl.BlockSpec(memory_space=pl.ANY)
    return pl.pallas_call(
        near_kernel,
        in_specs=[pl.BlockSpec(memory_space=pltpu.SMEM), vmem, vmem, anywhere] + [vmem] * 3,
        out_specs=(vmem, vmem, vmem),
        scratch_shapes=[
            pltpu.VMEM((2, count) + tensors.shape[2:], tensors.dtype),
            pltpu.SemaphoreType.DMA((2,)),
            pltpu.SemaphoreType.DMA((2,)),
        ],
        out_shape=(
            pltpu.VMEM((out_modes, groups * cells), jnp.float32),
            pltpu.VMEM((modes, groups * cells), jnp.float32),
            pltpu.VMEM((2, count) + tensors.shape[2:], tensors.dtype),
        ),
        compiler_params=pltpu.CompilerParams(vmem_limit_bytes=20 * MIB),
        cost_estimate=pl.CostEstimate(
            flops=tensors.size * groups * cells, transcendentals=0, bytes_accessed=tensors.size
        ),
        name="collide_near",
    )(table, close(mine), close(mate), tensors, close(one), close(two), close(three))


def far_kernel(
    table, one, two, tensors, early, next_, far, first, own, limiter, out, total, beside, sems
):
    last = copies_of(table, tensors, (2, 3), tensors.shape[1] - beside.shape[1], beside, sems)
    start_all(last)
    picks = [tensor_of(table, partner) for partner in (2, 3)]
    parts = [part_of(early, picks), part_of(next_, picks), part_of(far)]
    parts.append(part_of(beside, before=lambda: wait_all(last)))
    contract(parts, (one, two), own, total, first)
    groups, cells, _ = one.shape
    here = lax.axis_index("cell")
    whole = total[...].T
    out_modes = whole.shape[1]
    fold = fold_of(cells, out_modes)
    rows = cells // fold
    flag = limiter[:, cells - 1 :].astype(jnp.float32)
    spare = jnp.broadcast_to(flag, (rows, LANES - fold * out_modes))
    for d in range(groups):
        start = d * cells
        parts = [whole[start + f * rows : start + (f + 1) * rows] for f in range(fold)]
        out[here ^ reverse(d, groups)] = jnp.concatenate(parts + [spare], axis=1)


def collide_far(table, one, two, tensors, early, next_, far, first, own, limiter):
    groups, cells, modes = one.shape
    out_modes = tensors.shape[1]
    rows = cells // fold_of(cells, out_modes)
    left = out_modes - early.shape[1] - next_.shape[1] - far.shape[1]
    vmem = pl.BlockSpec(memory_space=pltpu.VMEM)
    anywhere = pl.BlockSpec(memory_space=pl.ANY)
    return pl.pallas_call(
        far_kernel,
        in_specs=[pl.BlockSpec(memory_space=pltpu.SMEM), vmem, vmem, anywhere] + [vmem] * 6,
        out_specs=vmem,
        scratch_shapes=[
            pltpu.VMEM((out_modes, groups * cells), jnp.float32),
            pltpu.VMEM((2, left) + tensors.shape[2:], tensors.dtype),
            pltpu.SemaphoreType.DMA((2,)),
        ],
        out_shape=pltpu.VMEM((groups, rows, LANES), jnp.float32),
        compiler_params=pltpu.CompilerParams(vmem_limit_bytes=20 * MIB),
        cost_estimate=pl.CostEstimate(
            flops=tensors.size * groups * cells, transcendentals=0, bytes_accessed=tensors.size
        ),
        name="collide_far",
    )(
        table,
        close(one),
        close(two),
        tensors,
        close(early),
        close(next_),
        close(far),
        close(first),
        close(own),
        limiter,
    )


def flux_kernel(mine, limiter, plus, minus, flux):
    groups, cells, modes = mine.shape
    place = lax.axis_index("cell")
    before = slot_of(place, lax.rem(place + groups - 1, groups), groups)
    after = slot_of(place, lax.rem(place + 1, groups), groups)
    wide = jnp.concatenate([mine[d].astype(jnp.float32) for d in (before, 0, after)], axis=0)
    wide = wide[cells - 2 : 2 * cells + 2]
    lower = wide[1:-1] - wide[:-2]
    upper = wide[2:] - wide[1:-1]
    one = minmod_two(lower, upper)
    two = minmod_three(2.0 * lower, 0.5 * (lower + upper), 2.0 * upper)
    flags = column(limiter[...])
    ahead = lax.broadcasted_iota(jnp.int32, (3, 1), 0)

    def chosen(first, second, flag):
        return jnp.where(flag == 1, first, jnp.where(flag == 2, second, 0.0))

    def stack(shift):
        base = wide[1 + shift :]
        faces = base[1 : cells + 1]
        faces = faces + (0.5 - shift) * chosen(
            one[1 + shift : 1 + shift + cells], two[1 + shift : 1 + shift + cells], flags
        )
        edge = base[:1] + (0.5 - shift) * chosen(
            one[shift : shift + 1], two[shift : shift + 1], ahead
        )
        pad = jnp.zeros((flux.shape[0] - cells - 3, modes), jnp.float32)
        return jnp.concatenate([faces, edge, pad], axis=0)

    total = jnp.dot(
        stack(0), plus[0], precision=lax.Precision.HIGHEST, preferred_element_type=jnp.float32
    )
    total = total + jnp.dot(
        stack(1), minus[0], precision=lax.Precision.HIGHEST, preferred_element_type=jnp.float32
    )
    flux[...] = total


def transport(mine, limiter, plus, minus):
    groups, cells, modes = mine.shape
    vmem = pl.BlockSpec(memory_space=pltpu.VMEM)
    return pl.pallas_call(
        flux_kernel,
        in_specs=[vmem, vmem, vmem, vmem],
        out_specs=vmem,
        out_shape=jax.ShapeDtypeStruct((cells + 8, modes), jnp.float32),
        compiler_params=pltpu.CompilerParams(vmem_limit_bytes=4 * MIB),
        name="transport",
    )(close(mine), limiter, plus, minus)


def finish_kernel(out_modes, received, flux, fields, new_field, collision):
    groups, rows, _ = received.shape
    cells = fields.shape[1]
    fold = cells // rows
    parts = []
    for f in range(fold):
        pieces = [received[g][:, f * out_modes : (f + 1) * out_modes] for g in range(groups)]
        parts.append(jnp.concatenate(pieces, axis=1))
    term = jnp.concatenate(parts, axis=0)
    collision[0] = term
    before = lax.rem(lax.axis_index("cell") + groups - 1, groups)
    flag = received[before][:1, fold * out_modes : fold * out_modes + 1]
    behind = flux[cells : cells + 3]
    edge = jnp.where(flag == 1.0, behind[1:2], jnp.where(flag == 2.0, behind[2:3], behind[:1]))
    faces = flux[:cells]
    ahead = jnp.concatenate([edge, faces[:-1]], axis=0)
    new_field[0] = fields[0].astype(jnp.float32) + 0.4 * (ahead - faces) + 0.5 * term


def finish(received, flux, fields, out_modes):
    vmem = pl.BlockSpec(memory_space=pltpu.VMEM)
    shape = jax.ShapeDtypeStruct(fields.shape, jnp.float32)
    return pl.pallas_call(
        functools.partial(finish_kernel, out_modes),
        in_specs=[vmem, vmem, vmem],
        out_specs=(vmem, vmem),
        out_shape=(shape, shape),
        compiler_params=pltpu.CompilerParams(vmem_limit_bytes=4 * MIB),
        name="finish",
    )(received, flux, fields)


def exchanged(x, axis, bit):
    return lax.ppermute(x, axis, [(i, i ^ bit) for i in range(lax.axis_size(axis))])


def local(fields, tensors, pair_table, plus_flux, minus_flux, face_limiter):
    groups = lax.axis_size("cell")
    count = tensors.shape[1] // SIXTHS
    mine, held, token = fields, [], None

    def more():
        first = len(held) * count
        if len(held) < 2:
            return fetch_all(mine if held else None, tensors, first, count)
        return fetch_near(pair_table, mine, tensors, first, 2 * count)

    bit = groups // 2
    while bit > 0:
        came = exchanged(mine, "cell", bit)
        if len(held) < 3:
            part, token = more()
            held.append(part)
        mine = join(mine, came, token)
        bit //= 2
    while len(held) < 3:
        held.append(more()[0])
    mate = exchanged(mine, "spec", 1)
    far_one = exchanged(mine, "spec", 2)
    far_two = exchanged(mate, "spec", 2)
    first, own, far = collide_near(pair_table, mine, mate, tensors, *held)
    block = collide_far(
        pair_table, far_one, far_two, tensors, held[0], held[1], far, first, own, face_limiter
    )
    received = lax.all_to_all(block, "cell", split_axis=0, concat_axis=0, tiled=False)
    flux = transport(mine, face_limiter, plus_flux, minus_flux)
    return finish(received, flux, fields, tensors.shape[1])


def solution(mesh):
    placed = (
        P("spec", "cell", None),
        P("spec", "cell", None, None),
        P(),
        P("spec", None, None),
        P("spec", None, None),
        P("spec", "cell"),
    )
    return jax.shard_map(
        local,
        mesh=mesh,
        in_specs=placed,
        out_specs=(P("spec", "cell", None), P("spec", "cell", None)),
        check_vma=False,
    )
```

```python
import functools

import jax
import jax.numpy as jnp
from jax import lax
from jax.experimental import pallas as pl
from jax.experimental.pallas import tpu as pltpu
from jax.sharding import PartitionSpec as P

LANES = 128
MIB = 1 << 20
SIXTHS = 6
NEAR = 7 * MIB
NEXT = 7 * MIB
FAR = 11 * MIB


def minmod_two(first, second):
    least = jnp.minimum(jnp.abs(first), jnp.abs(second))
    return jnp.where(first * second > 0, jnp.where(first > 0, least, -least), 0.0)


def minmod_three(first, second, third):
    same = (first * second > 0) & (second * third > 0)
    least = jnp.minimum(jnp.minimum(jnp.abs(first), jnp.abs(second)), jnp.abs(third))
    return jnp.where(same, jnp.where(first > 0, least, -least), 0.0)


def column(row):
    n = row.shape[1]
    down = lax.broadcasted_iota(jnp.int32, (n, n), 0)
    across = lax.broadcasted_iota(jnp.int32, (n, n), 1)
    return jnp.sum(jnp.where(down == across, row, 0), axis=1, keepdims=True)


def fold_of(cells, out_modes):
    fold = 1
    while cells % (2 * fold) == 0 and 2 * fold * out_modes < LANES:
        fold *= 2
    return fold


def reverse(number, count):
    out, bit = 0, 1
    while bit < count:
        out = out * 2 + number // bit % 2
        bit *= 2
    return out


def slot_of(here, there, groups):
    difference = here ^ there
    out, bit = 0, 0
    while (1 << bit) < groups:
        out = out * 2 + ((difference >> bit) & 1)
        bit += 1
    return out


def close(x):
    return pltpu.with_memory_space_constraint(x, pltpu.VMEM)


def tensor_of(table, partner):
    owner = lax.axis_index("spec")
    return table[owner, owner ^ partner] - owner * table.shape[0]


def copies_of(table, tensors, partners, first, near, sems):
    modes = pl.ds(first, near.shape[1])
    return [
        pltpu.make_async_copy(
            tensors.at[tensor_of(table, partner), modes], near.at[at], sems.at[at]
        )
        for at, partner in enumerate(partners)
    ]


def start_all(copies):
    for copy in copies:
        copy.start()


def wait_all(copies):
    for copy in copies:
        copy.wait()


def fetch_all_kernel(tensors, near, token, sem):
    copy = pltpu.make_async_copy(tensors.at[:, pl.ds(0, near.shape[1])], near, sem)
    copy.start()
    token[...] = jnp.zeros_like(token)
    copy.wait()


def fetch_near_kernel(table, after, tensors, near, token, sems, *, first):
    copies = copies_of(table, tensors, (0, 1), first, near, sems)
    start_all(copies)
    token[...] = jnp.zeros_like(token)
    wait_all(copies)


def fetch(kernel, operands, specs, tensors, species, count, sems):
    shape = (species, count) + tensors.shape[2:]
    vmem = pl.BlockSpec(memory_space=pltpu.VMEM)
    return pl.pallas_call(
        kernel,
        in_specs=specs + [pl.BlockSpec(memory_space=pl.ANY)],
        out_specs=(vmem, vmem),
        scratch_shapes=[sems],
        out_shape=(pltpu.VMEM(shape, tensors.dtype), pltpu.VMEM((8, LANES), jnp.float32)),
        compiler_params=pltpu.CompilerParams(vmem_limit_bytes=MIB),
        cost_estimate=pl.CostEstimate(
            flops=0,
            transcendentals=0,
            bytes_accessed=4 * species * count * tensors.shape[2] * tensors.shape[3],
        ),
        name="fetch",
    )(*operands, tensors)


def fetch_all(tensors, count):
    return fetch(
        fetch_all_kernel, [], [], tensors, tensors.shape[0], count, pltpu.SemaphoreType.DMA
    )


def fetch_near(table, after, tensors, first, count):
    specs = [pl.BlockSpec(memory_space=pltpu.SMEM), pl.BlockSpec(memory_space=pltpu.VMEM)]
    return fetch(
        functools.partial(fetch_near_kernel, first=first),
        [table, close(after)],
        specs,
        tensors,
        2,
        count,
        pltpu.SemaphoreType.DMA((2,)),
    )


def join_kernel(here, came, token, out):
    count = here.shape[0]
    out[:count] = here[...]
    out[count:] = came[...]


def join(here, came, token):
    vmem = pl.BlockSpec(memory_space=pltpu.VMEM)
    return pl.pallas_call(
        join_kernel,
        in_specs=[vmem, vmem, vmem],
        out_specs=vmem,
        out_shape=pltpu.VMEM((2 * here.shape[0],) + here.shape[1:], here.dtype),
        compiler_params=pltpu.CompilerParams(vmem_limit_bytes=MIB),
        name="join",
    )(close(here), close(came), close(token))


def contract(parts, others, own, total):
    groups, cells, modes = others[0].shape
    everyone = groups * cells
    width = 2 * LANES
    tiles = len(others) * modes // width
    spans = everyone // width

    def unit_of(pair, unit):
        at = 2 * pair + unit
        if spans == 1:
            return at, 0
        return at // spans, at % spans

    def columns_of(span):
        return slice(0, width) if spans == 1 else pl.ds(pl.multiple_of(span * width, width), width)

    def pieces_of(tile):
        for piece in (2 * tile, 2 * tile + 1):
            yield piece * LANES // modes, slice(piece * LANES % modes, piece * LANES % modes + LANES)

    def push(pair, tile, register):
        for unit in range(2):
            _, span = unit_of(pair, unit)
            of = width // cells
            rows = slice(0, of) if spans == 1 else pl.ds(span * of, of)
            tall = [others[p][rows, :, lanes].reshape(width, LANES) for p, lanes in pieces_of(tile)]
            pltpu.matmul_push_rhs(jnp.concatenate(tall, axis=1), register, unit, transpose=True)

    def run(*sums):
        def drain(part, pair, bank):
            for unit in range(2):
                k, span = unit_of(pair, unit)
                columns = columns_of(span)
                inner = pltpu.matmul_pop(sums[2 * unit + bank])
                row = jnp.sum(inner * own[:, columns], axis=0, keepdims=True)
                place = pl.ds(sum(count for _, count, _, _, _ in parts[:part]) + k, 1)
                add, shift = parts[part][3:]
                if add is not None:
                    row = row + add[pl.ds(shift + k, 1), columns]
                total[place, columns] = row

        def work(part, pair, bank, start, follower, pending):
            for tile in range(tiles):
                register = (start + tile) % 2
                if tile + 1 < tiles:
                    push(pair, tile + 1, 1 - register)
                elif follower is not None:
                    push(follower, 0, 1 - register)
                for unit in range(2):
                    k, _ = unit_of(pair, unit)
                    wide = [parts[part][0](p, k, lanes) for p, lanes in pieces_of(tile)]
                    pltpu.matmul_acc_lhs(
                        sums[2 * unit + bank], jnp.concatenate(wide, axis=1), register
                    )
                if tile == 0 and pending is not None:
                    drain(*pending)
            return (start + tiles) % 2

        pending, at = None, 0
        push(0, 0, at)
        for part in range(len(parts)):
            last = part + 1 == len(parts)
            pairs = parts[part][1] * spans // 2
            parts[part][2]()
            at = work(part, 0, 0, at, 1, pending)
            odd = at

            @pl.loop(0, (pairs - 2) // 2)
            def _(step):
                now = work(part, 2 * step + 1, 1, odd, 2 * step + 2, (part, 2 * step, 0))
                work(part, 2 * step + 2, 0, now, 2 * step + 3, (part, 2 * step + 1, 1))

            follower = None if last else 0
            at = work(part, pairs - 1, 1, odd, follower, (part, pairs - 2, 0))
            pending = (part, pairs - 1, 1)
        drain(*pending)

    pl.run_scoped(run, *[pltpu.ACC(unit)((modes, width), jnp.float32) for unit in (0, 0, 1, 1)])


def hold_kernel(x, after, out):
    out[...] = x[...]


def hold(x, after):
    vmem = pl.BlockSpec(memory_space=pltpu.VMEM)
    return pl.pallas_call(
        hold_kernel,
        in_specs=[vmem, vmem],
        out_specs=vmem,
        out_shape=pltpu.VMEM(x.shape, x.dtype),
        compiler_params=pltpu.CompilerParams(vmem_limit_bytes=MIB),
        name="hold",
    )(close(x), close(after))


def part_of(ref, picks=None, before=lambda: None, add=None, shift=0):
    def read(p, k, lanes):
        return ref[p if picks is None else picks[p], k, :, lanes]

    return read, ref.shape[1], before, add, shift


def near_kernel(table, mine, mate, tensors, shared, two, total, own, far, sems):
    later = copies_of(table, tensors, (2, 3), shared.shape[1], far, sems)
    start_all(later)
    own[...] = mine[...].reshape(own.shape[::-1]).astype(jnp.float32).T
    picks = [tensor_of(table, partner) for partner in (0, 1)]
    contract([part_of(shared, picks), part_of(two)], (mine, mate), own, total)
    wait_all(later)


def collide_near(table, mine, mate, tensors, shared, two):
    groups, cells, modes = mine.shape
    vmem = pl.BlockSpec(memory_space=pltpu.VMEM)
    anywhere = pl.BlockSpec(memory_space=pl.ANY)
    count = shared.shape[1] + two.shape[1]
    return pl.pallas_call(
        near_kernel,
        in_specs=[pl.BlockSpec(memory_space=pltpu.SMEM), vmem, vmem, anywhere, vmem, vmem],
        out_specs=(vmem, vmem, vmem),
        scratch_shapes=[pltpu.SemaphoreType.DMA((2,))],
        out_shape=(
            pltpu.VMEM((count, groups * cells), jnp.float32),
            pltpu.VMEM((modes, groups * cells), jnp.float32),
            pltpu.VMEM(two.shape, tensors.dtype),
        ),
        compiler_params=pltpu.CompilerParams(vmem_limit_bytes=NEAR),
        cost_estimate=pl.CostEstimate(
            flops=tensors.size // 2 * groups * cells,
            transcendentals=0,
            bytes_accessed=tensors.size // 2,
        ),
        name="collide_near",
    )(table, close(mine), close(mate), tensors, close(shared), close(two))


def next_kernel(
    table, after, mine, mate, tensors, three, own, total, far, beside, far_sems, sems
):
    count = beside.shape[1]
    last = copies_of(table, tensors, (0, 1), tensors.shape[1] - count, beside, sems)
    later = copies_of(table, tensors, (2, 3), tensors.shape[1] // 2, far, far_sems)
    start_all(last + later)
    parts = [part_of(three), part_of(beside, before=lambda: wait_all(last))]
    contract(parts, (mine, mate), own, total)
    wait_all(later)


def collide_next(table, after, mine, mate, tensors, three, own):
    groups, cells, modes = mine.shape
    vmem = pl.BlockSpec(memory_space=pltpu.VMEM)
    anywhere = pl.BlockSpec(memory_space=pl.ANY)
    count = tensors.shape[1] // 2
    few = (2, count - three.shape[1]) + tensors.shape[2:]
    return pl.pallas_call(
        next_kernel,
        in_specs=[pl.BlockSpec(memory_space=pltpu.SMEM)] + [vmem] * 3 + [anywhere, vmem, vmem],
        out_specs=(vmem, vmem),
        scratch_shapes=[
            pltpu.VMEM(few, tensors.dtype),
            pltpu.SemaphoreType.DMA((2,)),
            pltpu.SemaphoreType.DMA((2,)),
        ],
        out_shape=(
            pltpu.VMEM((count, groups * cells), jnp.float32),
            pltpu.VMEM(few, tensors.dtype),
        ),
        compiler_params=pltpu.CompilerParams(vmem_limit_bytes=NEXT),
        cost_estimate=pl.CostEstimate(
            flops=tensors.size // 2 * groups * cells,
            transcendentals=0,
            bytes_accessed=tensors.size // 2,
        ),
        name="collide_next",
    )(table, close(after), close(mine), close(mate), tensors, close(three), close(own))


def far_kernel(table, one, two, tensors, *refs):
    shared, far, more, first, second, own, limiter, out, total, beside, sems = refs
    last = copies_of(table, tensors, (2, 3), tensors.shape[1] - beside.shape[1], beside, sems)
    start_all(last)
    picks = [tensor_of(table, partner) for partner in (2, 3)]
    parts = [
        part_of(shared, picks, add=first),
        part_of(far, add=first, shift=shared.shape[1]),
        part_of(more, add=second),
        part_of(beside, before=lambda: wait_all(last), add=second, shift=more.shape[1]),
    ]
    contract(parts, (one, two), own, total)
    groups, cells, _ = one.shape
    here = lax.axis_index("cell")
    whole = total[...].T
    out_modes = whole.shape[1]
    fold = fold_of(cells, out_modes)
    rows = cells // fold
    flag = limiter[:, cells - 1 :].astype(jnp.float32)
    spare = jnp.broadcast_to(flag, (rows, LANES - fold * out_modes))
    for d in range(groups):
        start = d * cells
        parts = [whole[start + f * rows : start + (f + 1) * rows] for f in range(fold)]
        out[here ^ reverse(d, groups)] = jnp.concatenate(parts + [spare], axis=1)


def collide_far(table, one, two, tensors, shared, far, more, first, second, own, limiter):
    groups, cells, modes = one.shape
    out_modes = tensors.shape[1]
    rows = cells // fold_of(cells, out_modes)
    left = out_modes - shared.shape[1] - far.shape[1] - more.shape[1]
    vmem = pl.BlockSpec(memory_space=pltpu.VMEM)
    anywhere = pl.BlockSpec(memory_space=pl.ANY)
    return pl.pallas_call(
        far_kernel,
        in_specs=[pl.BlockSpec(memory_space=pltpu.SMEM), vmem, vmem, anywhere] + [vmem] * 7,
        out_specs=vmem,
        scratch_shapes=[
            pltpu.VMEM((out_modes, groups * cells), jnp.float32),
            pltpu.VMEM((2, left) + tensors.shape[2:], tensors.dtype),
            pltpu.SemaphoreType.DMA((2,)),
        ],
        out_shape=pltpu.VMEM((groups, rows, LANES), jnp.float32),
        compiler_params=pltpu.CompilerParams(vmem_limit_bytes=FAR),
        cost_estimate=pl.CostEstimate(
            flops=tensors.size * groups * cells, transcendentals=0, bytes_accessed=tensors.size
        ),
        name="collide_far",
    )(
        table,
        close(one),
        close(two),
        tensors,
        close(shared),
        close(far),
        close(more),
        close(first),
        close(second),
        close(own),
        limiter,
    )


def flux_kernel(mine, limiter, plus, minus, flux):
    groups, cells, modes = mine.shape
    place = lax.axis_index("cell")
    before = slot_of(place, lax.rem(place + groups - 1, groups), groups)
    after = slot_of(place, lax.rem(place + 1, groups), groups)
    wide = jnp.concatenate([mine[d].astype(jnp.float32) for d in (before, 0, after)], axis=0)
    wide = wide[cells - 2 : 2 * cells + 2]
    lower = wide[1:-1] - wide[:-2]
    upper = wide[2:] - wide[1:-1]
    one = minmod_two(lower, upper)
    two = minmod_three(2.0 * lower, 0.5 * (lower + upper), 2.0 * upper)
    flags = column(limiter[...])
    ahead = lax.broadcasted_iota(jnp.int32, (3, 1), 0)

    def chosen(first, second, flag):
        return jnp.where(flag == 1, first, jnp.where(flag == 2, second, 0.0))

    def stack(shift):
        base = wide[1 + shift :]
        faces = base[1 : cells + 1]
        faces = faces + (0.5 - shift) * chosen(
            one[1 + shift : 1 + shift + cells], two[1 + shift : 1 + shift + cells], flags
        )
        edge = base[:1] + (0.5 - shift) * chosen(
            one[shift : shift + 1], two[shift : shift + 1], ahead
        )
        pad = jnp.zeros((flux.shape[0] - cells - 3, modes), jnp.float32)
        return jnp.concatenate([faces, edge, pad], axis=0)

    total = jnp.dot(
        stack(0), plus[0], precision=lax.Precision.HIGHEST, preferred_element_type=jnp.float32
    )
    total = total + jnp.dot(
        stack(1), minus[0], precision=lax.Precision.HIGHEST, preferred_element_type=jnp.float32
    )
    flux[...] = total


def transport(mine, limiter, plus, minus):
    groups, cells, modes = mine.shape
    vmem = pl.BlockSpec(memory_space=pltpu.VMEM)
    return pl.pallas_call(
        flux_kernel,
        in_specs=[vmem, vmem, vmem, vmem],
        out_specs=vmem,
        out_shape=jax.ShapeDtypeStruct((cells + 8, modes), jnp.float32),
        compiler_params=pltpu.CompilerParams(vmem_limit_bytes=4 * MIB),
        name="transport",
    )(close(mine), limiter, plus, minus)


def finish_kernel(out_modes, received, flux, fields, new_field, collision):
    groups, rows, _ = received.shape
    cells = fields.shape[1]
    fold = cells // rows
    parts = []
    for f in range(fold):
        pieces = [received[g][:, f * out_modes : (f + 1) * out_modes] for g in range(groups)]
        parts.append(jnp.concatenate(pieces, axis=1))
    term = jnp.concatenate(parts, axis=0)
    collision[0] = term
    before = lax.rem(lax.axis_index("cell") + groups - 1, groups)
    flag = received[before][:1, fold * out_modes : fold * out_modes + 1]
    behind = flux[cells : cells + 3]
    edge = jnp.where(flag == 1.0, behind[1:2], jnp.where(flag == 2.0, behind[2:3], behind[:1]))
    faces = flux[:cells]
    ahead = jnp.concatenate([edge, faces[:-1]], axis=0)
    new_field[0] = fields[0].astype(jnp.float32) + 0.4 * (ahead - faces) + 0.5 * term


def finish(received, flux, fields, out_modes):
    vmem = pl.BlockSpec(memory_space=pltpu.VMEM)
    shape = jax.ShapeDtypeStruct(fields.shape, jnp.float32)
    return pl.pallas_call(
        functools.partial(finish_kernel, out_modes),
        in_specs=[vmem, vmem, vmem],
        out_specs=(vmem, vmem),
        out_shape=(shape, shape),
        compiler_params=pltpu.CompilerParams(vmem_limit_bytes=4 * MIB),
        name="finish",
    )(received, flux, fields)


def exchanged(x, axis, bit):
    return lax.ppermute(x, axis, [(i, i ^ bit) for i in range(lax.axis_size(axis))])


def local(fields, tensors, pair_table, plus_flux, minus_flux, face_limiter):
    groups = lax.axis_size("cell")
    count = tensors.shape[1] // SIXTHS
    mine, held, token = fields, [], None

    def more():
        if not held:
            return fetch_all(tensors, count)
        return fetch_near(pair_table, mine, tensors, (2 * len(held) - 1) * count, 2 * count)

    bit = groups // 2
    while bit > 0:
        came = exchanged(mine, "cell", bit)
        if len(held) < 3:
            part, token = more()
            held.append(part)
        mine = join(mine, came, token)
        bit //= 2
    while len(held) < 3:
        held.append(more()[0])
    mate = exchanged(mine, "spec", 1)
    far_one = exchanged(mine, "spec", 2)
    shared, two, three = held
    first, own, far = collide_near(pair_table, mine, mate, tensors, shared, two)
    far_one = hold(far_one, first)
    far_two = exchanged(far_one, "spec", 1)
    second, more_far = collide_next(pair_table, far_one, mine, mate, tensors, three, own)
    block = collide_far(
        pair_table,
        far_one,
        far_two,
        tensors,
        shared,
        far,
        more_far,
        first,
        second,
        own,
        face_limiter,
    )
    received = lax.all_to_all(block, "cell", split_axis=0, concat_axis=0, tiled=False)
    flux = transport(mine, face_limiter, plus_flux, minus_flux)
    return finish(received, flux, fields, tensors.shape[1])


def solution(mesh):
    placed = (
        P("spec", "cell", None),
        P("spec", "cell", None, None),
        P(),
        P("spec", None, None),
        P("spec", None, None),
        P("spec", "cell"),
    )
    return jax.shard_map(
        local,
        mesh=mesh,
        in_specs=placed,
        out_specs=(P("spec", "cell", None), P("spec", "cell", None)),
        check_vma=False,
    )
```

```python
import functools

import jax
import jax.numpy as jnp
from jax import lax
from jax.experimental import pallas as pl
from jax.experimental.pallas import tpu as pltpu
from jax.sharding import PartitionSpec as P

LANES = 128
MIB = 1 << 20
TWELFTHS = 12


def minmod_two(first, second):
    least = jnp.minimum(jnp.abs(first), jnp.abs(second))
    return jnp.where(first * second > 0, jnp.where(first > 0, least, -least), 0.0)


def minmod_three(first, second, third):
    same = (first * second > 0) & (second * third > 0)
    least = jnp.minimum(jnp.minimum(jnp.abs(first), jnp.abs(second)), jnp.abs(third))
    return jnp.where(same, jnp.where(first > 0, least, -least), 0.0)


def column(row):
    n = row.shape[1]
    down = lax.broadcasted_iota(jnp.int32, (n, n), 0)
    across = lax.broadcasted_iota(jnp.int32, (n, n), 1)
    return jnp.sum(jnp.where(down == across, row, 0), axis=1, keepdims=True)


def fold_of(cells, out_modes):
    fold = 1
    while cells % (2 * fold) == 0 and 2 * fold * out_modes < LANES:
        fold *= 2
    return fold


def reverse(number, count):
    out, bit = 0, 1
    while bit < count:
        out = out * 2 + number // bit % 2
        bit *= 2
    return out


def slot_of(here, there, groups):
    difference = here ^ there
    out, bit = 0, 0
    while (1 << bit) < groups:
        out = out * 2 + ((difference >> bit) & 1)
        bit += 1
    return out


def close(x):
    return pltpu.with_memory_space_constraint(x, pltpu.VMEM)


def tensor_of(table, partner):
    owner = lax.axis_index("spec")
    return table[owner, owner ^ partner] - owner * table.shape[0]


def copies_of(table, tensors, partners, first, near, sems):
    modes = pl.ds(first, near.shape[1])
    return [
        pltpu.make_async_copy(
            tensors.at[tensor_of(table, partner), modes], near.at[at], sems.at[at]
        )
        for at, partner in enumerate(partners)
    ]


def start_all(copies):
    for copy in copies:
        copy.start()


def wait_all(copies):
    for copy in copies:
        copy.wait()


def fetch_all_kernel(tensors, near, token, sem):
    copy = pltpu.make_async_copy(tensors.at[:, pl.ds(0, near.shape[1])], near, sem)
    copy.start()
    token[...] = jnp.zeros_like(token)
    copy.wait()


def fetch_near_kernel(table, after, tensors, near, token, sems, *, first):
    copies = copies_of(table, tensors, (0, 1), first, near, sems)
    start_all(copies)
    token[...] = jnp.zeros_like(token)
    wait_all(copies)


def fetch(kernel, operands, specs, tensors, species, count, sems):
    shape = (species, count) + tensors.shape[2:]
    vmem = pl.BlockSpec(memory_space=pltpu.VMEM)
    return pl.pallas_call(
        kernel,
        in_specs=specs + [pl.BlockSpec(memory_space=pl.ANY)],
        out_specs=(vmem, vmem),
        scratch_shapes=[sems],
        out_shape=(pltpu.VMEM(shape, tensors.dtype), pltpu.VMEM((8, LANES), jnp.float32)),
        compiler_params=pltpu.CompilerParams(vmem_limit_bytes=MIB),
        cost_estimate=pl.CostEstimate(
            flops=0,
            transcendentals=0,
            bytes_accessed=4 * species * count * tensors.shape[2] * tensors.shape[3],
        ),
        name="fetch",
    )(*operands, tensors)


def fetch_all(tensors, count):
    return fetch(
        fetch_all_kernel, [], [], tensors, tensors.shape[0], count, pltpu.SemaphoreType.DMA
    )


def fetch_near(table, after, tensors, first, count):
    specs = [pl.BlockSpec(memory_space=pltpu.SMEM), pl.BlockSpec(memory_space=pltpu.VMEM)]
    return fetch(
        functools.partial(fetch_near_kernel, first=first),
        [table, close(after)],
        specs,
        tensors,
        2,
        count,
        pltpu.SemaphoreType.DMA((2,)),
    )


def join_kernel(here, came, token, out):
    count = here.shape[0]
    out[:count] = here[...]
    out[count:] = came[...]


def join(here, came, token):
    vmem = pl.BlockSpec(memory_space=pltpu.VMEM)
    return pl.pallas_call(
        join_kernel,
        in_specs=[vmem, vmem, vmem],
        out_specs=vmem,
        out_shape=pltpu.VMEM((2 * here.shape[0],) + here.shape[1:], here.dtype),
        compiler_params=pltpu.CompilerParams(vmem_limit_bytes=MIB),
        name="join",
    )(close(here), close(came), close(token))


def contract(parts, others, own, total, add):
    groups, cells, modes = others[0].shape
    everyone = groups * cells
    width = 2 * LANES
    tiles = len(others) * modes // width
    spans = everyone // width

    def unit_of(pair, unit):
        at = 2 * pair + unit
        if spans == 1:
            return at, 0
        return at // spans, at % spans

    def columns_of(span):
        return slice(0, width) if spans == 1 else pl.ds(pl.multiple_of(span * width, width), width)

    def pieces_of(tile):
        for piece in (2 * tile, 2 * tile + 1):
            yield piece * LANES // modes, slice(piece * LANES % modes, piece * LANES % modes + LANES)

    def push(pair, tile, register):
        for unit in range(2):
            _, span = unit_of(pair, unit)
            of = width // cells
            rows = slice(0, of) if spans == 1 else pl.ds(span * of, of)
            tall = [others[p][rows, :, lanes].reshape(width, LANES) for p, lanes in pieces_of(tile)]
            pltpu.matmul_push_rhs(jnp.concatenate(tall, axis=1), register, unit, transpose=True)

    def run(*sums):
        def drain(part, pair, bank):
            for unit in range(2):
                k, span = unit_of(pair, unit)
                columns = columns_of(span)
                inner = pltpu.matmul_pop(sums[2 * unit + bank])
                row = jnp.sum(inner * own[:, columns], axis=0, keepdims=True)
                place = pl.ds(sum(count for _, count, _ in parts[:part]) + k, 1)
                total[place, columns] = row + add[place, columns] if add is not None else row

        def work(part, pair, bank, start, follower, pending):
            for tile in range(tiles):
                register = (start + tile) % 2
                if tile + 1 < tiles:
                    push(pair, tile + 1, 1 - register)
                elif follower is not None:
                    push(follower, 0, 1 - register)
                for unit in range(2):
                    k, _ = unit_of(pair, unit)
                    wide = [parts[part][0](p, k, lanes) for p, lanes in pieces_of(tile)]
                    pltpu.matmul_acc_lhs(
                        sums[2 * unit + bank], jnp.concatenate(wide, axis=1), register
                    )
                if tile == 0 and pending is not None:
                    drain(*pending)
            return (start + tiles) % 2

        pending, at = None, 0
        push(0, 0, at)
        for part in range(len(parts)):
            last = part + 1 == len(parts)
            pairs = parts[part][1] * spans // 2
            parts[part][2]()
            at = work(part, 0, 0, at, 1, pending)
            odd = at

            @pl.loop(0, (pairs - 2) // 2)
            def _(step):
                now = work(part, 2 * step + 1, 1, odd, 2 * step + 2, (part, 2 * step, 0))
                work(part, 2 * step + 2, 0, now, 2 * step + 3, (part, 2 * step + 1, 1))

            follower = None if last else 0
            at = work(part, pairs - 1, 1, odd, follower, (part, pairs - 2, 0))
            pending = (part, pairs - 1, 1)
        drain(*pending)

    pl.run_scoped(run, *[pltpu.ACC(unit)((modes, width), jnp.float32) for unit in (0, 0, 1, 1)])


def part_of(ref, picks=None, shift=0, count=None, before=lambda: None):
    def read(p, k, lanes):
        return ref[p if picks is None else picks[p], shift + k, :, lanes]

    return read, ref.shape[1] if count is None else count, before


def near_kernel(
    table, mine, mate, tensors, shared, two, three, total, own, far, beside, far_sems, sems
):
    first = shared.shape[1]
    last = copies_of(table, tensors, (0, 1), tensors.shape[1] - beside.shape[1], beside, sems)
    later = copies_of(table, tensors, (2, 3), first, far, far_sems)
    start_all(last + later)
    own[...] = mine[...].reshape(own.shape[::-1]).astype(jnp.float32).T
    picks = [tensor_of(table, partner) for partner in (0, 1)]
    parts = [part_of(shared, picks), part_of(two), part_of(three)]
    parts.append(part_of(beside, before=lambda: wait_all(last)))
    contract(parts, (mine, mate), own, total, None)
    wait_all(later)


def collide_near(table, mine, mate, tensors, shared, two, three):
    groups, cells, modes = mine.shape
    out_modes = tensors.shape[1]
    left = out_modes - shared.shape[1] - two.shape[1] - three.shape[1]
    ahead = 5 * out_modes // TWELFTHS
    vmem = pl.BlockSpec(memory_space=pltpu.VMEM)
    anywhere = pl.BlockSpec(memory_space=pl.ANY)
    return pl.pallas_call(
        near_kernel,
        in_specs=[pl.BlockSpec(memory_space=pltpu.SMEM), vmem, vmem, anywhere] + [vmem] * 3,
        out_specs=(vmem, vmem, vmem),
        scratch_shapes=[
            pltpu.VMEM((2, left) + tensors.shape[2:], tensors.dtype),
            pltpu.SemaphoreType.DMA((2,)),
            pltpu.SemaphoreType.DMA((2,)),
        ],
        out_shape=(
            pltpu.VMEM((out_modes, groups * cells), jnp.float32),
            pltpu.VMEM((modes, groups * cells), jnp.float32),
            pltpu.VMEM((2, ahead) + tensors.shape[2:], tensors.dtype),
        ),
        compiler_params=pltpu.CompilerParams(vmem_limit_bytes=7 * MIB),
        cost_estimate=pl.CostEstimate(
            flops=tensors.size * groups * cells, transcendentals=0, bytes_accessed=tensors.size
        ),
        name="collide_near",
    )(table, close(mine), close(mate), tensors, close(shared), close(two), close(three))


def far_kernel(
    table, one, two, tensors, shared, far, first, own, limiter, out, total, beside, sems
):
    last = copies_of(table, tensors, (2, 3), tensors.shape[1] - beside.shape[1], beside, sems)
    start_all(last)
    picks = [tensor_of(table, partner) for partner in (2, 3)]
    parts = [part_of(shared, picks), part_of(far)]
    parts.append(part_of(beside, before=lambda: wait_all(last)))
    contract(parts, (one, two), own, total, first)
    groups, cells, _ = one.shape
    here = lax.axis_index("cell")
    whole = total[...].T
    out_modes = whole.shape[1]
    fold = fold_of(cells, out_modes)
    rows = cells // fold
    flag = limiter[:, cells - 1 :].astype(jnp.float32)
    spare = jnp.broadcast_to(flag, (rows, LANES - fold * out_modes))
    for d in range(groups):
        start = d * cells
        parts = [whole[start + f * rows : start + (f + 1) * rows] for f in range(fold)]
        out[here ^ reverse(d, groups)] = jnp.concatenate(parts + [spare], axis=1)


def collide_far(table, one, two, tensors, shared, far, first, own, limiter):
    groups, cells, modes = one.shape
    out_modes = tensors.shape[1]
    rows = cells // fold_of(cells, out_modes)
    left = out_modes - shared.shape[1] - far.shape[1]
    vmem = pl.BlockSpec(memory_space=pltpu.VMEM)
    anywhere = pl.BlockSpec(memory_space=pl.ANY)
    return pl.pallas_call(
        far_kernel,
        in_specs=[pl.BlockSpec(memory_space=pltpu.SMEM), vmem, vmem, anywhere] + [vmem] * 5,
        out_specs=vmem,
        scratch_shapes=[
            pltpu.VMEM((out_modes, groups * cells), jnp.float32),
            pltpu.VMEM((2, left) + tensors.shape[2:], tensors.dtype),
            pltpu.SemaphoreType.DMA((2,)),
        ],
        out_shape=pltpu.VMEM((groups, rows, LANES), jnp.float32),
        compiler_params=pltpu.CompilerParams(vmem_limit_bytes=11 * MIB),
        cost_estimate=pl.CostEstimate(
            flops=tensors.size * groups * cells, transcendentals=0, bytes_accessed=tensors.size
        ),
        name="collide_far",
    )(
        table,
        close(one),
        close(two),
        tensors,
        close(shared),
        close(far),
        close(first),
        close(own),
        limiter,
    )


def flux_kernel(mine, limiter, plus, minus, flux):
    groups, cells, modes = mine.shape
    place = lax.axis_index("cell")
    before = slot_of(place, lax.rem(place + groups - 1, groups), groups)
    after = slot_of(place, lax.rem(place + 1, groups), groups)
    wide = jnp.concatenate([mine[d].astype(jnp.float32) for d in (before, 0, after)], axis=0)
    wide = wide[cells - 2 : 2 * cells + 2]
    lower = wide[1:-1] - wide[:-2]
    upper = wide[2:] - wide[1:-1]
    one = minmod_two(lower, upper)
    two = minmod_three(2.0 * lower, 0.5 * (lower + upper), 2.0 * upper)
    flags = column(limiter[...])
    ahead = lax.broadcasted_iota(jnp.int32, (3, 1), 0)

    def chosen(first, second, flag):
        return jnp.where(flag == 1, first, jnp.where(flag == 2, second, 0.0))

    def stack(shift):
        base = wide[1 + shift :]
        faces = base[1 : cells + 1]
        faces = faces + (0.5 - shift) * chosen(
            one[1 + shift : 1 + shift + cells], two[1 + shift : 1 + shift + cells], flags
        )
        edge = base[:1] + (0.5 - shift) * chosen(
            one[shift : shift + 1], two[shift : shift + 1], ahead
        )
        pad = jnp.zeros((flux.shape[0] - cells - 3, modes), jnp.float32)
        return jnp.concatenate([faces, edge, pad], axis=0)

    total = jnp.dot(
        stack(0), plus[0], precision=lax.Precision.HIGHEST, preferred_element_type=jnp.float32
    )
    total = total + jnp.dot(
        stack(1), minus[0], precision=lax.Precision.HIGHEST, preferred_element_type=jnp.float32
    )
    flux[...] = total


def transport(mine, limiter, plus, minus):
    groups, cells, modes = mine.shape
    vmem = pl.BlockSpec(memory_space=pltpu.VMEM)
    return pl.pallas_call(
        flux_kernel,
        in_specs=[vmem, vmem, vmem, vmem],
        out_specs=vmem,
        out_shape=jax.ShapeDtypeStruct((cells + 8, modes), jnp.float32),
        compiler_params=pltpu.CompilerParams(vmem_limit_bytes=4 * MIB),
        name="transport",
    )(close(mine), limiter, plus, minus)


def finish_kernel(out_modes, received, flux, fields, new_field, collision):
    groups, rows, _ = received.shape
    cells = fields.shape[1]
    fold = cells // rows
    parts = []
    for f in range(fold):
        pieces = [received[g][:, f * out_modes : (f + 1) * out_modes] for g in range(groups)]
        parts.append(jnp.concatenate(pieces, axis=1))
    term = jnp.concatenate(parts, axis=0)
    collision[0] = term
    before = lax.rem(lax.axis_index("cell") + groups - 1, groups)
    flag = received[before][:1, fold * out_modes : fold * out_modes + 1]
    behind = flux[cells : cells + 3]
    edge = jnp.where(flag == 1.0, behind[1:2], jnp.where(flag == 2.0, behind[2:3], behind[:1]))
    faces = flux[:cells]
    ahead = jnp.concatenate([edge, faces[:-1]], axis=0)
    new_field[0] = fields[0].astype(jnp.float32) + 0.4 * (ahead - faces) + 0.5 * term


def finish(received, flux, fields, out_modes):
    vmem = pl.BlockSpec(memory_space=pltpu.VMEM)
    shape = jax.ShapeDtypeStruct(fields.shape, jnp.float32)
    return pl.pallas_call(
        functools.partial(finish_kernel, out_modes),
        in_specs=[vmem, vmem, vmem],
        out_specs=(vmem, vmem),
        out_shape=(shape, shape),
        compiler_params=pltpu.CompilerParams(vmem_limit_bytes=4 * MIB),
        name="finish",
    )(received, flux, fields)


def exchanged(x, axis, bit):
    return lax.ppermute(x, axis, [(i, i ^ bit) for i in range(lax.axis_size(axis))])


def local(fields, tensors, pair_table, plus_flux, minus_flux, face_limiter):
    groups = lax.axis_size("cell")
    count = tensors.shape[1] // TWELFTHS
    mine, held, token = fields, [], None

    def more():
        if not held:
            return fetch_all(tensors, 3 * count)
        first = sum(part.shape[1] for part in held)
        return fetch_near(pair_table, mine, tensors, first, (2 + len(held)) * count)

    bit = groups // 2
    while bit > 0:
        came = exchanged(mine, "cell", bit)
        if len(held) < 3:
            part, token = more()
            held.append(part)
        mine = join(mine, came, token)
        bit //= 2
    while len(held) < 3:
        held.append(more()[0])
    mate = exchanged(mine, "spec", 1)
    far_one = exchanged(mine, "spec", 2)
    far_two = exchanged(mate, "spec", 2)
    first, own, far = collide_near(pair_table, mine, mate, tensors, *held)
    block = collide_far(
        pair_table, far_one, far_two, tensors, held[0], far, first, own, face_limiter
    )
    received = lax.all_to_all(block, "cell", split_axis=0, concat_axis=0, tiled=False)
    flux = transport(mine, face_limiter, plus_flux, minus_flux)
    return finish(received, flux, fields, tensors.shape[1])


def solution(mesh):
    placed = (
        P("spec", "cell", None),
        P("spec", "cell", None, None),
        P(),
        P("spec", None, None),
        P("spec", None, None),
        P("spec", "cell"),
    )
    return jax.shard_map(
        local,
        mesh=mesh,
        in_specs=placed,
        out_specs=(P("spec", "cell", None), P("spec", "cell", None)),
        check_vma=False,
    )
```
